32 devices in a mesh: grp: 2 (over y), sub: 4 (over z), chan: 4 (over x, core).
Axes of the slice: x: 2, y: 2, z: 4, core: 2. Of those that a mesh axis runs over, the one named last changes fastest.
Arguments:
- visibilities: bfloat16 [4, 32, 8, 2, 1024], P('chan', ('grp', 'sub')), parts along dimension 1, may hold values from -6 to 6
- tracks: float32 [32, 2, 128], P(('grp', 'sub')), parts along dimension 0, may hold values from -102 to 102
- freq_ratio: float32 [8, 64], P(('grp', 'chan')), parts along dimension 0, may hold values from 0.9 to 1.1
- blocks_used: int32 [32], P(('grp', 'sub')), parts along dimension 0, may hold values from 2 to 8, as said below
- subgrid_row: int32 [32], P(('grp', 'sub')), parts along dimension 0, may hold values from 0 to 15, as said below
- station_pair: int32 [32, 2], P(('grp', 'sub')), parts along dimension 0, may hold values from 0 to 127
- subgrid_offsets: int32 [32, 2], P(('grp', 'sub')), parts along dimension 0, may hold values from -90 to 90
- aterm_screens: bfloat16 [4, 256, 2, 1024], P('chan', ('grp', 'sub')), parts along dimension 1, may hold values from -4.1875 to 4.1875
Outputs:
- uv_subgrids: float32 [4, 32, 2, 1024], P('chan', ('grp', 'sub')), parts along dimension 1
The draws below stay inside these ranges and needn't reach their ends.
There are 2 independent parts, one for each index of `grp`. The reference program is written for one: setup_inputs(seed, part) draws one part's arguments, and reference() takes and returns one part's arrays. A program takes and returns all parts, laid end to end along the dimension named above; each array names one. Nothing has to cross between parts.
Inputs may be any that keep to these rules, and one draw needn't show every extreme that they name: `blocks_used`: time blocks from this count on hold no data and are left out. `subgrid_row`: A permutation of the 16 rows; row r lies on device r // 4 of sub. The used blocks of one device's baselines whose rows lie on one device number at most 8; the used blocks whose rows lie on one device number at most 26; one device's baselines hold at most 16 used blocks.
All inputs are finite; a program needn't handle non-finite values.
Results may differ from the reference program's by a relative error of at most 0.0047.
Values may be sent and summed in bfloat16 or wider, within the bound.
No kernel may reach another device: no remote copies, remote signals or barrier semaphores. Data moves between devices by JAX's collectives and lax.ppermute only.
A program may use at most 64 MiB of HBM per device.

```python
import math
import jax
import jax.numpy as jnp
from jax import lax

NST = 128
SUB = 32
PIX = 1024
CH = 64
TIME = 16
TB = 8
BPP = 1
K = 1024
NCB = 4
BL_DEV = 4
BL = 16


def shuffled(one_key):
    return jax.random.permutation(one_key, BL_DEV)


def layout(key):
    owners = BL // BL_DEV
    heavy_count = 3 * owners // 4
    keys = jax.random.split(jax.random.fold_in(key, 101), 5)
    owner_perm = jax.vmap(shuffled)(jax.random.split(keys[0], owners))
    target_owner = owner_perm // BPP
    heavy_owner = jax.random.randint(keys[1], (), 0, owners)
    heavy_source = jax.random.permutation(keys[2], owners) < heavy_count
    to_heavy = target_owner == heavy_owner
    bump_score = to_heavy.astype(jnp.int32) * BL_DEV + jax.vmap(shuffled)(jax.random.split(keys[3], owners))
    bump_rank = jnp.argsort(jnp.argsort(bump_score, axis=1), axis=1)
    bumped = (bump_rank < BL_DEV * 5 // 8) & jnp.logical_not(to_heavy)
    used = jnp.where(to_heavy & heavy_source[:, None], TB, jnp.where(bumped, 3, 2))
    row_score = target_owner.reshape(BL) * BL + jax.random.permutation(keys[4], BL)
    rows = jnp.argsort(jnp.argsort(row_score)).astype(jnp.int32)
    return (rows, used.reshape(BL).astype(jnp.int32))


def offset_table(key):
    return jax.random.randint(jax.random.fold_in(key, 202), (BL, 2), -90, 91).astype(jnp.int32)


def draw_blocks_used(key, part):
    rows, used = layout(key)
    return used


def draw_subgrid_row(key, part):
    rows, used = layout(key)
    return rows


def draw_subgrid_offsets(key, part):
    return offset_table(key)


def draw_tracks(key, part):
    rows, used = layout(key)
    offsets = offset_table(key)
    key = jax.random.fold_in(key, 303)
    keys = jax.random.split(key, 2)
    start = offsets[rows].astype(jnp.float32)
    speed = jax.random.uniform(keys[0], (BL, 2), jnp.float32, 1.5, 4.0) / TIME
    shift = jax.random.uniform(keys[1], (BL, 2), jnp.float32, -math.pi, math.pi)
    moments = jnp.arange(TB * TIME, dtype=jnp.float32)
    return start[:, :, None] + 10.0 * jnp.sin(shift[:, :, None] + speed[:, :, None] * moments[None, None, :])


def touch_ends(drawn, rng, low, top_value):
    longest = drawn.shape.index(max(drawn.shape))
    spots = []
    for shift in (0, 1):
        where = [jax.random.randint(jax.random.fold_in(rng, axis), (), 0, length) for axis, length in enumerate(drawn.shape)]
        where[longest] = (where[longest] + shift) % drawn.shape[longest]
        spots.append(tuple(where))
    return drawn.at[spots[0]].set(low).at[spots[1]].set(top_value)


def block_scale(stream_key, dims, pieces, least, high):
    factor_of, own = 1.0, jax.random.fold_in(stream_key, 6)
    for position, shards_of in pieces:
        steps = jnp.exp(jax.random.uniform(jax.random.fold_in(own, position), (shards_of,), jnp.float32, least / len(pieces), high / len(pieces)))
        factor_of = factor_of * jnp.repeat(steps, dims[position] // shards_of).reshape([-1 if axis == position else 1 for axis in range(len(dims))])
    return factor_of


def normal_values(own_key, dims, spread, bound, cuts=(), kind=jnp.bfloat16):
    result = spread * jax.random.normal(own_key, dims, jnp.float32)
    if cuts:
        result = result * block_scale(own_key, dims, cuts, -0.22, 0.18)
    return jnp.clip(result, -bound, bound).astype(kind)


def setup_inputs(seed: int = 0, part: int = 0) -> dict:
    arg_keys = jax.random.split(jax.random.key(seed), 9)
    part_splits = jax.random.split(jax.random.fold_in(arg_keys[8], part), 9)
    visibilities = normal_values(part_splits[0], (NCB, BL, TB, 2, K), 1.0, 6.0, ((0, 4), (1, 4)))
    tracks = draw_tracks(jax.random.fold_in(jax.random.fold_in(arg_keys[8], part), 71), part)
    freq_ratio = jnp.clip(0.9 + 0.20000005 * jax.random.uniform(part_splits[2], (NCB, CH), jnp.float32) ** block_scale(part_splits[2], (NCB, CH), ((0, 4),), -0.2, 0.2), 0.9, 1.1)
    blocks_used = draw_blocks_used(jax.random.fold_in(jax.random.fold_in(arg_keys[8], part), 71), part)
    subgrid_row = draw_subgrid_row(jax.random.fold_in(jax.random.fold_in(arg_keys[8], part), 71), part)
    station_pair = touch_ends(jax.random.randint(part_splits[5], (BL, 2), 0, NST), jax.random.fold_in(part_splits[5], 1), 0, NST - 1).astype(jnp.int32)
    subgrid_offsets = draw_subgrid_offsets(jax.random.fold_in(jax.random.fold_in(arg_keys[8], part), 71), part)
    aterm_screens = normal_values(part_splits[7], (NCB, NST, 2, PIX), 0.7, 4.1875, ((0, 4), (1, 4)))
    return {"visibilities": visibilities, "tracks": tracks, "freq_ratio": freq_ratio, "blocks_used": blocks_used, "subgrid_row": subgrid_row, "station_pair": station_pair, "subgrid_offsets": subgrid_offsets, "aterm_screens": aterm_screens}


TWO_PI = 2.0 * math.pi


def block_images(block_vis, block_tracks, centre, ratio_row):
    block_total = block_vis.shape[0]
    coords = jnp.arange(SUB, dtype=jnp.float32) - SUB // 2
    scaled = block_tracks[:, :, None, :] * ratio_row[None, None, :, None] - centre[:, :, None, None]
    phase_rate = (scaled * (TWO_PI / SUB)).reshape(block_total, 2, K)
    angles = phase_rate[:, :, None, :] * coords[None, None, :, None]
    cosine = jnp.cos(angles)
    sine_table = jnp.sin(angles)
    vis_real = block_vis[:, 0].astype(jnp.float32)[:, None, :]
    vis_imag = block_vis[:, 1].astype(jnp.float32)[:, None, :]
    left_real = (vis_real * cosine[:, 0] - vis_imag * sine_table[:, 0]).astype(jnp.bfloat16).astype(jnp.float32)
    left_imag = (vis_real * sine_table[:, 0] + vis_imag * cosine[:, 0]).astype(jnp.bfloat16).astype(jnp.float32)
    right_real = cosine[:, 1].astype(jnp.bfloat16).astype(jnp.float32)
    right_imag = sine_table[:, 1].astype(jnp.bfloat16).astype(jnp.float32)
    sum_real = jnp.einsum("glk,gmk->glm", left_real, right_real) - jnp.einsum("glk,gmk->glm", left_imag, right_imag)
    sum_imag = jnp.einsum("glk,gmk->glm", left_real, right_imag) + jnp.einsum("glk,gmk->glm", left_imag, right_real)
    norm_scale = K ** -0.5
    image_real = (sum_real * norm_scale).reshape(block_total, PIX)
    image_imag = (sum_imag * norm_scale).reshape(block_total, PIX)
    return jnp.stack([image_real, image_imag], axis=1).astype(jnp.bfloat16)


def make_taper():
    coords = jnp.arange(SUB, dtype=jnp.float32) - SUB // 2
    taper_line = 1.0 - (2.0 * coords / (SUB + 2)) ** 2
    return (taper_line[:, None] * taper_line[None, :]).reshape(PIX)


def apply_terms(subgrids, first_screen, second_screen, taper_map):
    tap_real = subgrids[:, 0] * taper_map
    tap_imag = subgrids[:, 1] * taper_map
    gain_real = first_screen[:, 0] * second_screen[:, 0] + first_screen[:, 1] * second_screen[:, 1]
    gain_imag = first_screen[:, 0] * second_screen[:, 1] - first_screen[:, 1] * second_screen[:, 0]
    return jnp.stack([tap_real * gain_real - tap_imag * gain_imag, tap_real * gain_imag + tap_imag * gain_real], axis=1)


def transform(weighted):
    rows_total = weighted.shape[0]
    planes = weighted.reshape(rows_total, 2, SUB, SUB)
    field = lax.complex(planes[:, 0], planes[:, 1])
    spectrum = jnp.fft.fftshift(jnp.fft.fft2(jnp.fft.ifftshift(field, axes=(1, 2)), axes=(1, 2)), axes=(1, 2)) / SUB
    return jnp.stack([jnp.real(spectrum), jnp.imag(spectrum)], axis=1).reshape(rows_total, 2, PIX).astype(jnp.float32)


def reference(visibilities, tracks, freq_ratio, blocks_used, subgrid_row, station_pair, subgrid_offsets, aterm_screens):
    group_size = 4
    row_centres = subgrid_offsets[subgrid_row].astype(jnp.float32)
    split_tracks = tracks.reshape(BL, 2, TB, TIME).transpose(0, 2, 1, 3)
    used_mask = jnp.arange(TB, dtype=jnp.int32)[None, :] < blocks_used[:, None]
    row_pairs = jnp.zeros((BL, 2), jnp.int32).at[subgrid_row].set(station_pair)
    taper_map = make_taper()

    def one_band(band):
        band_vis, band_ratio, band_screens = band

        def one_group(group_items):
            group_vis, group_tracks, group_centre, group_mask = group_items
            flat_centre = jnp.broadcast_to(group_centre[:, None, :], (group_size, TB, 2)).reshape(group_size * TB, 2)
            images = block_images(group_vis.reshape(group_size * TB, 2, K), group_tracks.reshape(group_size * TB, 2, TIME), flat_centre, band_ratio)
            images = images.reshape(group_size, TB, 2, PIX).astype(jnp.float32)
            return jnp.sum(jnp.where(group_mask[:, :, None, None], images, 0.0), axis=1)

        count = BL // group_size
        sums = lax.map(one_group, (band_vis.reshape(count, group_size, TB, 2, K), split_tracks.reshape(count, group_size, TB, 2, TIME), row_centres.reshape(count, group_size, 2), used_mask.reshape(count, group_size, TB)))
        sums = sums.reshape(BL, 2, PIX)
        subgrids = jnp.zeros((BL, 2, PIX), jnp.float32).at[subgrid_row].set(sums)
        first_screen = band_screens[row_pairs[:, 0]].astype(jnp.float32)
        second_screen = band_screens[row_pairs[:, 1]].astype(jnp.float32)
        weighted = apply_terms(subgrids, first_screen, second_screen, taper_map)
        return transform(weighted)

    return lax.map(one_band, (visibilities, freq_ratio, aterm_screens))
```

```python
import functools
import math

import jax
import jax.numpy as jnp
from jax import lax
from jax.experimental import pallas as pl
from jax.experimental.pallas import tpu as pltpu
from jax.sharding import PartitionSpec as P

SUB = 32
LANES = 128
SLOTS = LANES // SUB
QROWS = SUB // SLOTS
META = 16
TWO_PI = 2.0 * math.pi
HIGHEST = lax.Precision.HIGHEST


def turn_cos_sin(turns):
    part = turns - jnp.round(turns)
    square = part * part
    sine = part * (
        3.14159264 + square * (-5.16771008 + square * (2.55007752 + square * (-0.59829129 + square * 0.07765766)))
    )
    cosine = 0.99999995 + square * (
        -4.93479283 + square * (4.05841135 + square * (-1.33187657 + square * 0.21968961))
    )
    return 1.0 - 2.0 * sine * sine, 2.0 * sine * cosine


def times(a_real, a_imag, b_real, b_imag):
    return a_real * b_real - a_imag * b_imag, a_real * b_imag + a_imag * b_real


def iota(shape, axis):
    return lax.broadcasted_iota(jnp.int32, shape, axis)


def image_kernel(axis_size, used_ref, row_ref, pair_ref, vis_ref, tracks_ref, freq_ref, *rest):
    send_refs, (lines_ref, turns_ref, powers_ref, total_ref) = rest[:-4], rest[-4:]
    base_count, blocks, _, samples = vis_ref.shape[1:]
    channels = freq_ref.shape[1]
    steps = samples // channels
    me = lax.axis_index("sub")
    lines = 2 * base_count

    for b in range(base_count):
        lines_ref[2 * b : 2 * b + 2, :] = tracks_ref[b]
    spread = (iota((channels, samples), 1) // steps == iota((channels, samples), 0)).astype(jnp.float32)
    ratio = jnp.dot(
        jnp.broadcast_to(freq_ref[...], (8, channels)), spread, precision=HIGHEST, preferred_element_type=jnp.float32
    )[0:1]
    most = used_ref[0]
    for b in range(1, base_count):
        most = jnp.maximum(most, used_ref[b])

    def prepare(j, _):
        pick = iota((blocks * steps, samples), 0) == j * steps + iota((blocks * steps, samples), 1) % steps
        moved = jnp.dot(
            lines_ref[...], pick.astype(jnp.float32), precision=HIGHEST, preferred_element_type=jnp.float32
        )
        turns = moved * ratio * (1.0 / SUB)
        turns = turns - jnp.round(turns)
        turns_ref[j] = turns
        weight = jnp.where(iota((lines, 1), 0) % 2 == 0, 1.0, float(QROWS))
        one = turn_cos_sin(turns * weight)
        two = times(*one, *one)
        three = times(*two, *one)
        for power, (real, imag) in enumerate((one, two, three)):
            powers_ref[j, 2 * power] = real
            powers_ref[j, 2 * power + 1] = imag
        return 0

    lax.fori_loop(0, most, prepare, 0)
    total_ref[...] = jnp.zeros_like(total_ref)
    q_start = (iota((QROWS, 1), 0) * SLOTS - SUB // 2).astype(jnp.float32)
    r_start = (iota((QROWS, 1), 0) - SUB // 2).astype(jnp.float32)
    for b in range(base_count):

        def one_block(j, sums):
            sample = vis_ref[0, b, j].astype(jnp.float32)

            def fan(real, imag, line):
                reals, imags = [real], [imag]
                for power in range(SLOTS - 1):
                    power_real = powers_ref[j, 2 * power, line : line + 1, :]
                    power_imag = powers_ref[j, 2 * power + 1, line : line + 1, :]
                    next_real, next_imag = times(real, imag, power_real, power_imag)
                    reals.append(next_real)
                    imags.append(next_imag)
                return jnp.concatenate(reals + imags, axis=0).astype(jnp.bfloat16)

            base = turn_cos_sin(turns_ref[j, 2 * b : 2 * b + 1, :] * q_start)
            left = fan(*times(*base, sample[0:1], sample[1:2]), 2 * b)
            right = fan(*turn_cos_sin(turns_ref[j, 2 * b + 1 : 2 * b + 2, :] * r_start), 2 * b + 1)
            return sums + lax.dot_general(left, right, (((1,), (1,)), ((), ())), preferred_element_type=jnp.float32)

        sums = lax.fori_loop(0, used_ref[b], one_block, jnp.zeros((2 * SUB, 2 * SUB), jnp.float32))
        real = sums[:SUB, :SUB] - sums[SUB:, SUB:]
        imag = sums[:SUB, SUB:] + sums[SUB:, :SUB]
        image = jnp.concatenate([real, imag], axis=0) * samples**-0.5
        stations = iota((META, SUB), 0)
        stations = jnp.where(stations == 0, pair_ref[b, 0], jnp.where(stations == 1, pair_ref[b, 1], 0))
        image = jnp.concatenate([image, stations.astype(jnp.float32)], axis=0)
        image = jnp.concatenate([image, jnp.zeros((image.shape[0], LANES - SUB), jnp.float32)], axis=1)
        row = row_ref[b]
        owner = row // base_count
        slot = row % base_count
        place = lax.rem(owner - me + axis_size, axis_size)
        image = pltpu.roll(image, (slot % SLOTS) * SUB, 1)
        total_ref[place, slot // SLOTS] += image
    if len(send_refs) == 1:
        send_refs[0][...] = total_ref[...].astype(jnp.bfloat16)
    else:
        for place, send_ref in enumerate(send_refs):
            send_ref[...] = total_ref[place].astype(jnp.bfloat16)


def gather_kernel(offset_ref, *rest):
    payload_refs, (pixels_ref, station_ref) = rest[:-2], rest[-2:]
    groups = pixels_ref.shape[0] // SLOTS
    for g in range(groups):
        parts = []
        for ref in payload_refs:
            parts += [ref[g]] if len(ref.shape) == 3 else [ref[p, g] for p in range(ref.shape[0])]
        whole = parts[0].astype(jnp.float32)
        for part in parts[1:]:
            whole = whole + part.astype(jnp.float32)
        lane = iota((QROWS, LANES), 1)
        q = iota((QROWS, LANES), 0) * SLOTS + lane // SUB - SUB // 2
        r = lane % SUB - SUB // 2
        line = lambda h: 1.0 - (2.0 * h.astype(jnp.float32) / (SUB + 2)) ** 2
        taper = line(q) * line(r)
        names = whole[2 * SUB : 2 * SUB + 8].astype(jnp.int32)
        for s in range(SLOTS):
            slot = g * SLOTS + s
            flat = []
            for c in range(2):
                value = jnp.zeros((QROWS, LANES), jnp.float32)
                for i in range(SLOTS):
                    start = c * SUB + i * QROWS
                    moved = pltpu.roll(whole[start : start + QROWS], ((i - s) % SLOTS) * SUB, 1)
                    value = jnp.where(lane // SUB == i, moved, value)
                flat.append(value)
            turn = lax.rem(offset_ref[slot, 0] * q + offset_ref[slot, 1] * r, SUB)
            cosine, sine = turn_cos_sin(turn.astype(jnp.float32) * (1.0 / SUB))
            real, imag = times(*flat, cosine * taper, -sine * taper)
            pixels_ref[slot, 0] = real
            pixels_ref[slot, 1] = imag
            for e in range(2):
                station_ref[slot, e] = names[e, s * SUB]


def finish_kernel(station_ref, pixels_ref, screens_ref, out_ref, picked_ref, rows_ref, sems):
    base_count = pixels_ref.shape[0]
    copies = []
    for n in range(2 * base_count):
        copy = pltpu.make_async_copy(
            screens_ref.at[0, station_ref[n // 2, n % 2]], picked_ref.at[n], sems.at[n]
        )
        copy.start()
        copies.append(copy)
    order = lambda n: (n % QROWS) * SLOTS + n // QROWS - SUB // 2
    size = (LANES, LANES)
    same = iota(size, 0) // SUB == iota(size, 1) // SUB
    turn = (iota(size, 0) % SUB - SUB // 2) * (iota(size, 1) % SUB - SUB // 2)
    r_cos, r_sin = turn_cos_sin(turn.astype(jnp.float32) * (1.0 / SUB))
    r_table = jnp.concatenate([jnp.where(same, r_cos, 0.0), jnp.where(same, r_sin, 0.0)], axis=1)
    size = (SUB, SUB)
    q_cos, q_sin = turn_cos_sin((order(iota(size, 0)) * order(iota(size, 1))).astype(jnp.float32) * (1.0 / SUB))
    q_table = jnp.concatenate(
        [jnp.concatenate([q_cos, q_sin], axis=1), jnp.concatenate([-q_sin, q_cos], axis=1)], axis=0
    ) * (1.0 / SUB)
    lane = iota((QROWS, LANES), 1)
    for copy in copies:
        copy.wait()
    for g in range(base_count // SLOTS):
        weighted = []
        for s in range(SLOTS):
            slot = g * SLOTS + s
            screens = []
            for e in range(2):
                n = 2 * slot + e
                value = picked_ref[n].astype(jnp.float32)
                for a in range(QROWS):
                    rows_ref[n, 2 * a : 2 * a + 2, :] = value[:, a * LANES : (a + 1) * LANES]
                screens.append((rows_ref[n, pl.ds(0, QROWS, stride=2), :], rows_ref[n, pl.ds(1, QROWS, stride=2), :]))
            (p_real, p_imag), (s_real, s_imag) = screens
            gain = times(p_real, -p_imag, s_real, s_imag)
            weighted.append(times(pixels_ref[slot, 0], pixels_ref[slot, 1], *gain))
        planes = []
        for c in range(2):
            for i in range(SLOTS):
                value = jnp.zeros((QROWS, LANES), jnp.float32)
                for s in range(SLOTS):
                    moved = pltpu.roll(weighted[s][c], ((s - i) % SLOTS) * SUB, 1)
                    value = jnp.where(lane // SUB == s, moved, value)
                planes.append(value)
        planes = jnp.concatenate(planes, axis=0)
        half = jnp.dot(planes, r_table, precision=HIGHEST, preferred_element_type=jnp.float32)
        half_real = half[:SUB, :LANES] + half[SUB:, LANES:]
        half_imag = half[SUB:, :LANES] - half[:SUB, LANES:]
        half = jnp.concatenate([half_real, half_imag], axis=0)
        full = jnp.dot(q_table, half, precision=HIGHEST, preferred_element_type=jnp.float32)
        for s in range(SLOTS):
            for c in range(2):
                value = jnp.zeros((QROWS, LANES), jnp.float32)
                for i in range(SLOTS):
                    start = c * SUB + i * QROWS
                    moved = pltpu.roll(full[start : start + QROWS], ((i - s) % SLOTS) * SUB, 1)
                    value = jnp.where(lane // SUB == i, moved, value)
                for a in range(QROWS):
                    out_ref[0, g * SLOTS + s, c : c + 1, a * LANES : (a + 1) * LANES] = value[a : a + 1]


def local(
    visibilities, tracks, freq_ratio, blocks_used, subgrid_row, station_pair, subgrid_offsets, aterm_screens
):
    owners = lax.axis_size("sub")
    base_count, blocks, _, samples = visibilities.shape[1:]
    groups = -(-base_count // SLOTS)
    pixels = aterm_screens.shape[-1]
    rows = 2 * SUB + META
    vmem = pl.BlockSpec(memory_space=pltpu.VMEM)
    smem = pl.BlockSpec(memory_space=pltpu.SMEM)
    screens = lax.all_gather(aterm_screens, "sub", axis=1, tiled=True)
    direct = owners <= 8
    if direct:
        sends = [jax.ShapeDtypeStruct((groups, rows, LANES), jnp.bfloat16)] * owners
    else:
        sends = [jax.ShapeDtypeStruct((owners, groups, rows, LANES), jnp.bfloat16)]
    sent = pl.pallas_call(
        functools.partial(image_kernel, owners),
        out_shape=sends,
        in_specs=[smem, smem, smem, vmem, vmem, vmem],
        out_specs=[vmem] * len(sends),
        scratch_shapes=[
            pltpu.VMEM((2 * base_count, tracks.shape[-1]), jnp.float32),
            pltpu.VMEM((blocks, 2 * base_count, samples), jnp.float32),
            pltpu.VMEM((blocks, 2 * (SLOTS - 1), 2 * base_count, samples), jnp.float32),
            pltpu.VMEM((owners, groups, rows, LANES), jnp.float32),
        ],
        compiler_params=pltpu.CompilerParams(vmem_limit_bytes=48 * 1024 * 1024),
        name="images",
    )(blocks_used, subgrid_row, station_pair, visibilities, tracks, freq_ratio)
    if direct:
        payloads = [sent[0]]
        for shift in range(1, owners):
            payloads.append(lax.ppermute(sent[shift], "sub", [(n, (n + shift) % owners) for n in range(owners)]))
    else:
        here = lax.axis_index("sub")
        payloads = [lax.all_to_all(jnp.roll(sent[0], here, axis=0), "sub", 0, 0, tiled=True)]
    subgrids, stations = pl.pallas_call(
        gather_kernel,
        out_shape=[
            jax.ShapeDtypeStruct((base_count, 2, QROWS, LANES), jnp.float32),
            jax.ShapeDtypeStruct((base_count, 2), jnp.int32),
        ],
        in_specs=[smem] + [vmem] * len(payloads),
        out_specs=[vmem, smem],
        compiler_params=pltpu.CompilerParams(vmem_limit_bytes=48 * 1024 * 1024),
        name="subgrids",
    )(subgrid_offsets, *payloads)
    return pl.pallas_call(
        finish_kernel,
        out_shape=jax.ShapeDtypeStruct((1, base_count, 2, pixels), jnp.float32),
        in_specs=[smem, vmem, pl.BlockSpec(memory_space=pl.ANY)],
        out_specs=vmem,
        scratch_shapes=[
            pltpu.VMEM((2 * base_count, 2, pixels), jnp.bfloat16),
            pltpu.VMEM((2 * base_count, 2 * QROWS, LANES), jnp.float32),
            pltpu.SemaphoreType.DMA((2 * base_count,)),
        ],
        compiler_params=pltpu.CompilerParams(vmem_limit_bytes=48 * 1024 * 1024),
        name="finish",
    )(stations, subgrids, screens)


def solution(mesh):
    in_specs = (
        P("chan", ("grp", "sub"), None, None, None),
        P(("grp", "sub"), None, None),
        P(("grp", "chan"), None),
        P(("grp", "sub")),
        P(("grp", "sub")),
        P(("grp", "sub"), None),
        P(("grp", "sub"), None),
        P("chan", ("grp", "sub"), None, None),
    )
    out_specs = P("chan", ("grp", "sub"), None, None)
    return jax.shard_map(local, mesh=mesh, in_specs=in_specs, out_specs=out_specs, check_vma=False)
```

```python
import functools
import math

import jax
import jax.numpy as jnp
from jax import lax
from jax.experimental import pallas as pl
from jax.experimental.pallas import tpu as pltpu
from jax.sharding import PartitionSpec as P

SUB = 32
LANES = 128
SLOTS = LANES // SUB
QROWS = SUB // SLOTS
ROWS = 2 * SUB + 16
HIGHEST = lax.Precision.HIGHEST
SINE = (3.14159027, -5.16740673, 2.54401052, -0.55946246)
COSINE = (0.99999325, -4.93393467, 4.0412481, -1.22203176)
SINE_LONG = (3.14159264, -5.16771008, 2.55007752, -0.59829129, 0.07765766)
COSINE_LONG = (0.99999995, -4.93479283, 4.05841135, -1.33187657, 0.21968961)


def series(terms, square):
    value = terms[-1]
    for term in terms[-2::-1]:
        value = term + square * value
    return value


def turn_cos_sin(turns, sine_terms=SINE_LONG, cosine_terms=COSINE_LONG):
    part = turns - jnp.round(turns)
    square = part * part
    sine = part * series(sine_terms, square)
    twice = sine + sine
    return 1.0 - twice * sine, twice * series(cosine_terms, square)


def times(a_real, a_imag, b_real, b_imag):
    return a_real * b_real - a_imag * b_imag, a_real * b_imag + a_imag * b_real


def iota(shape, axis):
    return lax.broadcasted_iota(jnp.int32, shape, axis)


def image_kernel(
    axis_size, used_hbm, row_hbm, pair_hbm, vis_hbm, tracks_hbm, freq_hbm, *rest
):
    send_refs, scratch = rest[:-13], rest[-13:]
    (used_ref, row_ref, pair_ref, vis_ref, tracks_ref, freq_ref, lines_ref, turns_ref, powers_ref, total_ref,
     sems, wide_ref, image_ref) = scratch
    base_count, blocks, _, samples = vis_ref.shape
    channels = freq_ref.shape[1]
    steps = samples // channels
    groups = -(-base_count // SLOTS)
    me = lax.axis_index("sub")
    lines = 2 * base_count
    tiles = samples // LANES
    sources = (
        (tracks_hbm, tracks_ref), (freq_hbm, freq_ref), (used_hbm, used_ref), (vis_hbm.at[0], vis_ref),
        (row_hbm, row_ref), (pair_hbm, pair_ref),
    )
    copies = [pltpu.make_async_copy(one, two, sems.at[n]) for n, (one, two) in enumerate(sources)]
    for copy in copies:
        copy.start()
    copies[0].wait()
    copies[1].wait()
    for b in range(base_count):
        lines_ref[2 * b : 2 * b + 2, :] = tracks_ref[b]
    wide_ref[...] = jnp.zeros_like(wide_ref)
    wide_ref[0:1, :channels] = freq_ref[...]
    wide = jnp.broadcast_to(wide_ref[0:1, :], (8, LANES))
    lane = iota((8, LANES), 1)
    ratio = jnp.concatenate(
        [jnp.take_along_axis(wide, (lane + m * LANES) // steps, axis=1) for m in range(tiles)], axis=1
    )[0:1] * (1.0 / SUB)
    weight = jnp.where(iota((lines, 1), 0) % 2 == 0, 1.0, float(QROWS))

    def prepare(j, _):
        moved = jnp.take_along_axis(lines_ref[...], iota((lines, LANES), 1) % steps + j * steps, axis=1)
        turns = jnp.concatenate([moved] * tiles, axis=1) * ratio
        turns = turns - jnp.round(turns)
        turns_ref[j] = turns
        one = turn_cos_sin(turns * weight, SINE, COSINE)
        two = times(*one, *one)
        three = times(*two, *one)
        for power, (real, imag) in enumerate((one, two, three)):
            powers_ref[j, 2 * power] = real
            powers_ref[j, 2 * power + 1] = imag
        return 0

    lax.fori_loop(0, blocks, prepare, 0, unroll=2)
    total_ref[...] = jnp.zeros_like(total_ref)
    q_start = (iota((QROWS, 1), 0) * SLOTS - SUB // 2).astype(jnp.float32)
    r_start = (iota((QROWS, 1), 0) - SUB // 2).astype(jnp.float32)
    for copy in copies[2:]:
        copy.wait()
    for b in range(base_count):

        def one_block(j):
            sample = vis_ref[b, j].astype(jnp.float32)
            sample = jnp.where(j < used_ref[b], sample, 0.0)

            def fan(real, imag, line):
                reals, imags = [real], [imag]
                for power in range(SLOTS - 1):
                    power_real = powers_ref[j, 2 * power, line : line + 1, :]
                    power_imag = powers_ref[j, 2 * power + 1, line : line + 1, :]
                    next_real, next_imag = times(real, imag, power_real, power_imag)
                    reals.append(next_real)
                    imags.append(next_imag)
                return jnp.concatenate(reals + imags, axis=0).astype(jnp.bfloat16)

            base = turn_cos_sin(turns_ref[j, 2 * b : 2 * b + 1, :] * q_start, SINE, COSINE)
            left = fan(*times(*base, sample[0:1], sample[1:2]), 2 * b)
            right = fan(*turn_cos_sin(turns_ref[j, 2 * b + 1 : 2 * b + 2, :] * r_start, SINE, COSINE), 2 * b + 1)
            return lax.dot_general(left, right, (((1,), (1,)), ((), ())), preferred_element_type=jnp.float32)

        def two_blocks(half, sums):
            return sums + one_block(2 * half) + one_block(2 * half + 1)

        sums = lax.fori_loop(0, (used_ref[b] + 1) // 2, two_blocks, jnp.zeros((2 * SUB, 2 * SUB), jnp.float32))
        real = sums[:SUB, :SUB] - sums[SUB:, SUB:]
        imag = sums[:SUB, SUB:] + sums[SUB:, :SUB]
        image_ref[0:SUB, 0:SUB] = real * samples**-0.5
        image_ref[SUB : 2 * SUB, 0:SUB] = imag * samples**-0.5
        stations = iota((ROWS - 2 * SUB, LANES), 0)
        stations = jnp.where(stations == 0, pair_ref[0, b], jnp.where(stations == 1, pair_ref[1, b], 0))
        image_ref[2 * SUB :, :] = stations.astype(jnp.float32)
        image = jnp.where(iota((ROWS, LANES), 1) < SUB, image_ref[...], 0.0)
        row = row_ref[b]
        owner = row // base_count
        slot = row % base_count
        place = lax.rem(owner - me + axis_size, axis_size)
        total_ref[place, slot // SLOTS] += pltpu.roll(image, (slot % SLOTS) * SUB, 1)
    if len(send_refs) > 1:
        for place, send_ref in enumerate(send_refs):
            send_ref[...] = total_ref[place].astype(jnp.bfloat16)
    else:
        send_refs[0][...] = total_ref[...].astype(jnp.bfloat16)


def split_rows(value, rows_ref, first):
    for a in range(value.shape[1] // LANES):
        rows_ref[first + 2 * a : first + 2 * a + 2, :] = value[:, a * LANES : (a + 1) * LANES]


def swap(parts, lane):
    swapped = []
    for s in range(SLOTS):
        value = parts[s]
        for i in range(SLOTS):
            if i != s:
                value = jnp.where(lane // SUB == i, pltpu.roll(parts[i], ((i - s) % SLOTS) * SUB, 1), value)
        swapped.append(value)
    return swapped


def finish_kernel(payload_count, offset_hbm, table_hbm, *rest):
    payload_refs = rest[:payload_count]
    screens_refs = rest[payload_count:-6]
    out_ref, offset_ref, table_ref, rows_ref, screen_ref, sems = rest[-6:]
    copies = [
        pltpu.make_async_copy(offset_hbm, offset_ref, sems.at[0]),
        pltpu.make_async_copy(table_hbm, table_ref, sems.at[1]),
    ]
    for copy in copies:
        copy.start()
    base_count = out_ref.shape[1]
    groups = -(-base_count // SLOTS)
    me = lax.axis_index("sub")
    owners = lax.axis_size("sub")
    lane = iota((QROWS, LANES), 1)
    q = iota((QROWS, LANES), 0) * SLOTS + lane // SUB - SUB // 2
    r = lane % SUB - SUB // 2
    line = lambda h: 1.0 - (2.0 * h.astype(jnp.float32) / (SUB + 2)) ** 2
    taper = line(q) * line(r)

    def screen(station):
        if len(screens_refs) == 1:
            return screens_refs[0][0, station]
        here = screens_refs[0].shape[1]
        sent_from = station // here
        away = me ^ sent_from
        parts = [ref[0, station - sent_from * here] if len(ref.shape) == 4 else ref[station - sent_from * here] for ref in screens_refs]
        value = parts[0]
        for shift in range(1, owners):
            value = jnp.where(away == shift, parts[shift], value)
        return value

    for g in range(groups):
        parts = []
        for ref in payload_refs:
            parts += [ref[g]] if len(ref.shape) == 3 else [ref[p, g] for p in range(ref.shape[0])]
        whole = parts[0].astype(jnp.float32)
        for part in parts[1:]:
            whole = whole + part.astype(jnp.float32)
        rows_ref[...] = whole
        names = rows_ref[2 * SUB : 2 * SUB + 8, :].astype(jnp.int32)
        gains = []
        for s in range(SLOTS):
            pair = []
            for e in range(2):
                n = 2 * s + e
                split_rows(screen(names[e, s * SUB]).astype(jnp.float32), screen_ref.at[n], 0)
                pair.append((screen_ref[n, pl.ds(0, QROWS, stride=2), :], screen_ref[n, pl.ds(1, QROWS, stride=2), :]))
            (p_real, p_imag), (s_real, s_imag) = pair
            gains.append(times(p_real, -p_imag, s_real, s_imag))
        real = swap([rows_ref[i * QROWS : (i + 1) * QROWS, :] for i in range(SLOTS)], lane)
        imag = swap([rows_ref[SUB + i * QROWS : SUB + (i + 1) * QROWS, :] for i in range(SLOTS)], lane)
        if g == 0:
            for copy in copies:
                copy.wait()
        weighted = []
        for s in range(SLOTS):
            slot = g * SLOTS + s
            turn = lax.rem(offset_ref[0, slot] * q + offset_ref[1, slot] * r, SUB)
            cosine, sine = turn_cos_sin(turn.astype(jnp.float32) * (1.0 / SUB))
            centred = times(real[s], imag[s], cosine * taper, -sine * taper)
            weighted.append(times(*centred, *gains[s]))
        planes = swap([pair[0] for pair in weighted], lane) + swap([pair[1] for pair in weighted], lane)
        planes = jnp.concatenate(planes, axis=0)
        half = jnp.dot(planes, table_ref[:LANES], precision=HIGHEST, preferred_element_type=jnp.float32)
        half_real = half[:SUB, :LANES] + half[SUB:, LANES:]
        half_imag = half[SUB:, :LANES] - half[:SUB, LANES:]
        half = jnp.concatenate([half_real, half_imag], axis=0)
        full = jnp.dot(table_ref[LANES:, : 2 * SUB], half, precision=HIGHEST, preferred_element_type=jnp.float32)
        for c in range(2):
            flat = swap([full[c * SUB + i * QROWS : c * SUB + (i + 1) * QROWS] for i in range(SLOTS)], lane)
            for s in range(SLOTS):
                for a in range(QROWS):
                    out_ref[0, g * SLOTS + s, c : c + 1, a * LANES : (a + 1) * LANES] = flat[s][a : a + 1]


def tables():
    h = [n - SUB // 2 for n in range(SUB)]
    order = [(n % QROWS) * SLOTS + n // QROWS - SUB // 2 for n in range(SUB)]
    turn = lambda f, x, y: f(2.0 * math.pi * ((x * y) % SUB) / SUB)
    r_table = [
        [turn(f, h[m % SUB], h[n % SUB]) if m // SUB == n // SUB else 0.0 for f in (math.cos, math.sin) for n in range(LANES)]
        for m in range(LANES)
    ]
    cos = [[turn(math.cos, x, y) / SUB for y in order] for x in order]
    sin = [[turn(math.sin, x, y) / SUB for y in order] for x in order]
    q_table = [c + s for c, s in zip(cos, sin)] + [[-v for v in s] + c for c, s in zip(cos, sin)]
    return jnp.array(r_table + [row + [0.0] * (2 * LANES - 2 * SUB) for row in q_table], jnp.float32)


def local(
    visibilities, tracks, freq_ratio, blocks_used, subgrid_row, station_pair, subgrid_offsets, aterm_screens
):
    owners = lax.axis_size("sub")
    base_count, blocks, _, samples = visibilities.shape[1:]
    groups = -(-base_count // SLOTS)
    here, _, pixels = aterm_screens.shape[1:]
    vmem = pl.BlockSpec(memory_space=pltpu.VMEM)
    hbm = pl.BlockSpec(memory_space=pltpu.HBM)
    keep = lambda x: pltpu.with_memory_space_constraint(x, pltpu.HBM)
    shift_by = lambda x, shift: lax.ppermute(x, "sub", [(n, (n + shift) % owners) for n in range(owners)])
    direct = owners == 4
    if direct:
        flip = lambda x, bits: lax.ppermute(x, "sub", [(n, n ^ bits) for n in range(owners)])
        screens = [aterm_screens, flip(aterm_screens, 1), flip(aterm_screens, 2)]
        sends = [jax.ShapeDtypeStruct((groups, ROWS, LANES), jnp.bfloat16)] * owners
    else:
        sends = [jax.ShapeDtypeStruct((owners, groups, ROWS, LANES), jnp.bfloat16)]
    sent = pl.pallas_call(
        functools.partial(image_kernel, owners),
        out_shape=sends,
        in_specs=[hbm] * 6,
        out_specs=[vmem] * len(sends),
        scratch_shapes=[
            pltpu.SMEM((base_count,), jnp.int32),
            pltpu.SMEM((base_count,), jnp.int32),
            pltpu.SMEM((2, base_count), jnp.int32),
            pltpu.VMEM(visibilities.shape[1:], jnp.bfloat16),
            pltpu.VMEM(tracks.shape, jnp.float32),
            pltpu.VMEM(freq_ratio.shape, jnp.float32),
            pltpu.VMEM((2 * base_count, tracks.shape[-1]), jnp.float32),
            pltpu.VMEM((blocks, 2 * base_count, samples), jnp.float32),
            pltpu.VMEM((blocks, 2 * (SLOTS - 1), 2 * base_count, samples), jnp.float32),
            pltpu.VMEM((owners, groups, ROWS, LANES), jnp.float32),
            pltpu.SemaphoreType.DMA((6,)),
            pltpu.VMEM((8, LANES), jnp.float32),
            pltpu.VMEM((ROWS, LANES), jnp.float32),
        ],
        compiler_params=pltpu.CompilerParams(vmem_limit_bytes=48 * 1024 * 1024),
        name="images",
    )(*map(keep, (blocks_used, subgrid_row, station_pair.T, visibilities, tracks, freq_ratio)))
    if direct:
        sent, screens[2] = lax.optimization_barrier((list(sent), screens[2]))
        screens.append(flip(screens[2], 1))
        payloads = [sent[0]] + [shift_by(sent[shift], shift) for shift in range(1, owners)]
    else:
        by_owner = jnp.roll(sent[0], lax.axis_index("sub"), axis=0)
        payloads = [lax.all_to_all(by_owner, "sub", 0, 0, tiled=True)]
        screens = [lax.all_gather(aterm_screens, "sub", axis=1, tiled=True)]
    return pl.pallas_call(
        functools.partial(finish_kernel, len(payloads)),
        out_shape=jax.ShapeDtypeStruct((1, base_count, 2, pixels), jnp.float32),
        in_specs=[hbm] * 2 + [vmem] * (len(payloads) + len(screens)),
        out_specs=vmem,
        scratch_shapes=[
            pltpu.SMEM((2, base_count), jnp.int32),
            pltpu.VMEM((LANES + 2 * SUB, 2 * LANES), jnp.float32),
            pltpu.VMEM((ROWS, LANES), jnp.float32),
            pltpu.VMEM((2 * SLOTS, 2 * QROWS, LANES), jnp.float32),
            pltpu.SemaphoreType.DMA((2,)),
        ],
        compiler_params=pltpu.CompilerParams(vmem_limit_bytes=48 * 1024 * 1024),
        name="finish",
    )(keep(subgrid_offsets.T), keep(tables()), *payloads, *screens)


def solution(mesh):
    in_specs = (
        P("chan", ("grp", "sub"), None, None, None),
        P(("grp", "sub"), None, None),
        P(("grp", "chan"), None),
        P(("grp", "sub")),
        P(("grp", "sub")),
        P(("grp", "sub"), None),
        P(("grp", "sub"), None),
        P("chan", ("grp", "sub"), None, None),
    )
    out_specs = P("chan", ("grp", "sub"), None, None)
    return jax.shard_map(local, mesh=mesh, in_specs=in_specs, out_specs=out_specs, check_vma=False)
```

```python
import functools
import math

import jax
import jax.numpy as jnp
from jax import lax
from jax.experimental import pallas as pl
from jax.experimental.pallas import tpu as pltpu
from jax.sharding import PartitionSpec as P

SUB = 32
LANES = 128
SLOTS = LANES // SUB
QROWS = SUB // SLOTS
ROWS = 2 * SUB + 16
STEP = 8
HIGHEST = lax.Precision.HIGHEST
SINE = (3.14159027, -5.16740673, 2.54401052, -0.55946246)
COSINE = (0.99999325, -4.93393467, 4.0412481, -1.22203176)
SINE_LONG = (3.14159264, -5.16771008, 2.55007752, -0.59829129, 0.07765766)
COSINE_LONG = (0.99999995, -4.93479283, 4.05841135, -1.33187657, 0.21968961)


def series(terms, square):
    value = terms[-1]
    for term in terms[-2::-1]:
        value = term + square * value
    return value


def turn_cos_sin(turns, sine_terms=SINE_LONG, cosine_terms=COSINE_LONG):
    part = turns - jnp.round(turns)
    square = part * part
    sine = part * series(sine_terms, square)
    twice = sine + sine
    return 1.0 - twice * sine, twice * series(cosine_terms, square)


def times(a_real, a_imag, b_real, b_imag):
    return a_real * b_real - a_imag * b_imag, a_real * b_imag + a_imag * b_real


def iota(shape, axis):
    return lax.broadcasted_iota(jnp.int32, shape, axis)


def image_kernel(
    axis_size, used_hbm, row_hbm, pair_hbm, vis_hbm, tracks_hbm, freq_hbm, *rest
):
    send_refs, scratch = rest[:-15], rest[-15:]
    (used_ref, row_ref, pair_ref, vis_ref, tracks_ref, freq_ref, lines_ref, turns_ref, powers_ref, total_ref,
     sems, wide_ref, image_ref, sums_ref, block_ref) = scratch
    base_count, blocks, _, samples = vis_ref.shape
    channels = freq_ref.shape[1]
    steps = samples // channels
    groups = -(-base_count // SLOTS)
    me = lax.axis_index("sub")
    lines = 2 * base_count
    tiles = samples // LANES
    sources = (
        (tracks_hbm, tracks_ref), (freq_hbm, freq_ref), (used_hbm, used_ref), (vis_hbm.at[0], vis_ref),
        (row_hbm, row_ref), (pair_hbm, pair_ref),
    )
    copies = [pltpu.make_async_copy(one, two, sems.at[n]) for n, (one, two) in enumerate(sources)]
    for copy in copies:
        copy.start()
    copies[0].wait()
    copies[1].wait()
    for b in range(base_count):
        lines_ref[2 * b : 2 * b + 2, :] = tracks_ref[b]
    wide_ref[...] = jnp.zeros_like(wide_ref)
    wide_ref[0:1, :channels] = freq_ref[...]
    wide = jnp.broadcast_to(wide_ref[0:1, :], (8, LANES))
    lane = iota((8, LANES), 1)
    ratio = jnp.concatenate(
        [jnp.take_along_axis(wide, (lane + m * LANES) // steps, axis=1) for m in range(tiles)], axis=1
    )[0:1] * (1.0 / SUB)
    weight = jnp.where(iota((lines, 1), 0) % 2 == 0, 1.0, float(QROWS))

    def prepare(j, _):
        moved = jnp.take_along_axis(lines_ref[...], iota((lines, LANES), 1) % steps + j * steps, axis=1)
        turns = jnp.concatenate([moved] * tiles, axis=1) * ratio
        turns = turns - jnp.round(turns)
        turns_ref[j] = turns
        one = turn_cos_sin(turns * weight, SINE, COSINE)
        two = times(*one, *one)
        three = times(*two, *one)
        for power, (real, imag) in enumerate((one, two, three)):
            powers_ref[j, 2 * power] = real
            powers_ref[j, 2 * power + 1] = imag
        return 0

    lax.fori_loop(0, blocks, prepare, 0, unroll=2)
    total_ref[...] = jnp.zeros_like(total_ref)
    sums_ref[...] = jnp.zeros_like(sums_ref)
    q_start = (iota((QROWS, 1), 0) * SLOTS - SUB // 2).astype(jnp.float32)
    r_start = (iota((QROWS, 1), 0) - SUB // 2).astype(jnp.float32)
    for copy in copies[2:]:
        copy.wait()

    count = jnp.int32(0)
    for b in range(base_count):

        def note(j, _):
            block_ref[count + j] = b * blocks + j
            return 0

        lax.fori_loop(0, used_ref[b], note, 0)
        count = count + used_ref[b]
    for n in range(STEP - 1):
        block_ref[count + n] = 0

    def some_blocks(step, _):
        for n in range(STEP):
            block = block_ref[step * STEP + n]
            b, j = block // blocks, block % blocks
            sample = vis_ref[b, j].astype(jnp.float32)
            sample = jnp.where(step * STEP + n < count, sample, 0.0)

            def fan(real, imag, line):
                reals, imags = [real], [imag]
                for power in range(SLOTS - 1):
                    power_real = powers_ref[j, 2 * power, pl.ds(line, 1), :]
                    power_imag = powers_ref[j, 2 * power + 1, pl.ds(line, 1), :]
                    next_real, next_imag = times(real, imag, power_real, power_imag)
                    reals.append(next_real)
                    imags.append(next_imag)
                return jnp.concatenate(reals + imags, axis=0).astype(jnp.bfloat16)

            turns = [turns_ref[j, pl.ds(2 * b + axis, 1), :] for axis in range(2)]
            base = turn_cos_sin(turns[0] * q_start, SINE, COSINE)
            left = fan(*times(*base, sample[0:1], sample[1:2]), 2 * b)
            right = fan(*turn_cos_sin(turns[1] * r_start, SINE, COSINE), 2 * b + 1)
            sums_ref[b] += lax.dot_general(left, right, (((1,), (1,)), ((), ())), preferred_element_type=jnp.float32)
        return 0

    lax.fori_loop(0, (count + STEP - 1) // STEP, some_blocks, 0)
    for b in range(base_count):
        sums = sums_ref[b]
        real = sums[:SUB, :SUB] - sums[SUB:, SUB:]
        imag = sums[:SUB, SUB:] + sums[SUB:, :SUB]
        image_ref[0:SUB, 0:SUB] = real * samples**-0.5
        image_ref[SUB : 2 * SUB, 0:SUB] = imag * samples**-0.5
        stations = iota((ROWS - 2 * SUB, LANES), 0)
        stations = jnp.where(stations == 0, pair_ref[0, b], jnp.where(stations == 1, pair_ref[1, b], 0))
        image_ref[2 * SUB :, :] = stations.astype(jnp.float32)
        image = jnp.where(iota((ROWS, LANES), 1) < SUB, image_ref[...], 0.0)
        row = row_ref[b]
        owner = row // base_count
        slot = row % base_count
        place = lax.rem(owner - me + axis_size, axis_size)
        total_ref[place, slot // SLOTS] += pltpu.roll(image, (slot % SLOTS) * SUB, 1)
    if len(send_refs) > 1:
        for place, send_ref in enumerate(send_refs):
            send_ref[...] = total_ref[place].astype(jnp.bfloat16)
    else:
        send_refs[0][...] = total_ref[...].astype(jnp.bfloat16)


def split_rows(value, rows_ref, first):
    for a in range(value.shape[1] // LANES):
        rows_ref[first + 2 * a : first + 2 * a + 2, :] = value[:, a * LANES : (a + 1) * LANES]


def swap(parts, lane):
    swapped = []
    for s in range(SLOTS):
        value = parts[s]
        for i in range(SLOTS):
            if i != s:
                value = jnp.where(lane // SUB == i, pltpu.roll(parts[i], ((i - s) % SLOTS) * SUB, 1), value)
        swapped.append(value)
    return swapped


def subgrid_kernel(offset_hbm, table_hbm, *rest):
    payload_refs, (pixels_ref, station_ref, table_ref, offset_ref, rows_ref, sems) = rest[:-6], rest[-6:]
    copy = pltpu.make_async_copy(offset_hbm, offset_ref, sems.at[0])
    copy.start()
    table_copy = pltpu.make_async_copy(table_hbm, table_ref, sems.at[1])
    table_copy.start()
    lane = iota((QROWS, LANES), 1)
    q = iota((QROWS, LANES), 0) * SLOTS + lane // SUB - SUB // 2
    r = lane % SUB - SUB // 2
    line = lambda h: 1.0 - (2.0 * h.astype(jnp.float32) / (SUB + 2)) ** 2
    taper = line(q) * line(r)
    for g in range(pixels_ref.shape[0] // SLOTS):
        parts = []
        for ref in payload_refs:
            parts += [ref[g]] if len(ref.shape) == 3 else [ref[p, g] for p in range(ref.shape[0])]
        whole = parts[0].astype(jnp.float32)
        for part in parts[1:]:
            whole = whole + part.astype(jnp.float32)
        rows_ref[...] = whole
        station_ref[g] = rows_ref[2 * SUB : 2 * SUB + 8, :].astype(jnp.int32)
        real = swap([rows_ref[i * QROWS : (i + 1) * QROWS, :] for i in range(SLOTS)], lane)
        imag = swap([rows_ref[SUB + i * QROWS : SUB + (i + 1) * QROWS, :] for i in range(SLOTS)], lane)
        if g == 0:
            copy.wait()
        for s in range(SLOTS):
            slot = g * SLOTS + s
            turn = lax.rem(offset_ref[0, slot] * q + offset_ref[1, slot] * r, SUB)
            cosine, sine = turn_cos_sin(turn.astype(jnp.float32) * (1.0 / SUB))
            pixels_ref[slot, 0], pixels_ref[slot, 1] = times(real[s], imag[s], cosine * taper, -sine * taper)
    table_copy.wait()


def finish_kernel(table_ref, station_ref, pixels_ref, *rest):
    screens_refs, (out_ref, screen_ref) = rest[:-2], rest[-2:]
    me = lax.axis_index("sub")
    lane = iota((QROWS, LANES), 1)

    def screen(station):
        if len(screens_refs) == 1:
            return screens_refs[0][0, station]
        here = screens_refs[0].shape[1]
        away = me ^ (station // here)
        value = screens_refs[0][0, station % here]
        for flips in range(1, len(screens_refs)):
            value = jnp.where(away == flips, screens_refs[flips][0, station % here], value)
        return value

    for g in range(pixels_ref.shape[0] // SLOTS):
        weighted = []
        names = station_ref[g]
        for s in range(SLOTS):
            slot = g * SLOTS + s
            pair = []
            for e in range(2):
                n = 2 * s + e
                split_rows(screen(names[e, s * SUB]).astype(jnp.float32), screen_ref.at[n], 0)
                pair.append((screen_ref[n, pl.ds(0, QROWS, stride=2), :], screen_ref[n, pl.ds(1, QROWS, stride=2), :]))
            (p_real, p_imag), (s_real, s_imag) = pair
            gain = times(p_real, -p_imag, s_real, s_imag)
            weighted.append(times(pixels_ref[slot, 0], pixels_ref[slot, 1], *gain))
        planes = swap([pair[0] for pair in weighted], lane) + swap([pair[1] for pair in weighted], lane)
        planes = jnp.concatenate(planes, axis=0)
        half = jnp.dot(planes, table_ref[:LANES], precision=HIGHEST, preferred_element_type=jnp.float32)
        half_real = half[:SUB, :LANES] + half[SUB:, LANES:]
        half_imag = half[SUB:, :LANES] - half[:SUB, LANES:]
        half = jnp.concatenate([half_real, half_imag], axis=0)
        full = jnp.dot(table_ref[LANES:, : 2 * SUB], half, precision=HIGHEST, preferred_element_type=jnp.float32)
        for c in range(2):
            flat = swap([full[c * SUB + i * QROWS : c * SUB + (i + 1) * QROWS] for i in range(SLOTS)], lane)
            for s in range(SLOTS):
                for a in range(QROWS):
                    out_ref[0, g * SLOTS + s, c : c + 1, a * LANES : (a + 1) * LANES] = flat[s][a : a + 1]


def tables():
    h = [n - SUB // 2 for n in range(SUB)]
    order = [(n % QROWS) * SLOTS + n // QROWS - SUB // 2 for n in range(SUB)]
    turn = lambda f, x, y: f(2.0 * math.pi * ((x * y) % SUB) / SUB)
    r_table = [
        [turn(f, h[m % SUB], h[n % SUB]) if m // SUB == n // SUB else 0.0 for f in (math.cos, math.sin) for n in range(LANES)]
        for m in range(LANES)
    ]
    cos = [[turn(math.cos, x, y) / SUB for y in order] for x in order]
    sin = [[turn(math.sin, x, y) / SUB for y in order] for x in order]
    q_table = [c + s for c, s in zip(cos, sin)] + [[-v for v in s] + c for c, s in zip(cos, sin)]
    return jnp.array(r_table + [row + [0.0] * (2 * LANES - 2 * SUB) for row in q_table], jnp.float32)


def local(
    visibilities, tracks, freq_ratio, blocks_used, subgrid_row, station_pair, subgrid_offsets, aterm_screens
):
    owners = lax.axis_size("sub")
    base_count, blocks, _, samples = visibilities.shape[1:]
    groups = -(-base_count // SLOTS)
    here, _, pixels = aterm_screens.shape[1:]
    vmem = pl.BlockSpec(memory_space=pltpu.VMEM)
    hbm = pl.BlockSpec(memory_space=pltpu.HBM)
    keep = lambda x: pltpu.with_memory_space_constraint(x, pltpu.HBM)
    shift_by = lambda x, shift: lax.ppermute(x, "sub", [(n, (n + shift) % owners) for n in range(owners)])
    direct = owners == 4
    if direct:
        flip = lambda x, bits: lax.ppermute(x, "sub", [(n, n ^ bits) for n in range(owners)])
        screens = [aterm_screens, flip(aterm_screens, 1), flip(aterm_screens, 2)]
        sends = [jax.ShapeDtypeStruct((groups, ROWS, LANES), jnp.bfloat16)] * owners
    else:
        sends = [jax.ShapeDtypeStruct((owners, groups, ROWS, LANES), jnp.bfloat16)]
    sent = pl.pallas_call(
        functools.partial(image_kernel, owners),
        out_shape=sends,
        in_specs=[hbm] * 6,
        out_specs=[vmem] * len(sends),
        scratch_shapes=[
            pltpu.SMEM((base_count,), jnp.int32),
            pltpu.SMEM((base_count,), jnp.int32),
            pltpu.SMEM((2, base_count), jnp.int32),
            pltpu.VMEM(visibilities.shape[1:], jnp.bfloat16),
            pltpu.VMEM(tracks.shape, jnp.float32),
            pltpu.VMEM(freq_ratio.shape, jnp.float32),
            pltpu.VMEM((2 * base_count, tracks.shape[-1]), jnp.float32),
            pltpu.VMEM((blocks, 2 * base_count, samples), jnp.float32),
            pltpu.VMEM((blocks, 2 * (SLOTS - 1), 2 * base_count, samples), jnp.float32),
            pltpu.VMEM((owners, groups, ROWS, LANES), jnp.float32),
            pltpu.SemaphoreType.DMA((6,)),
            pltpu.VMEM((8, LANES), jnp.float32),
            pltpu.VMEM((ROWS, LANES), jnp.float32),
            pltpu.VMEM((base_count, 2 * SUB, 2 * SUB), jnp.float32),
            pltpu.SMEM((base_count * blocks + STEP - 1,), jnp.int32),
        ],
        compiler_params=pltpu.CompilerParams(vmem_limit_bytes=48 * 1024 * 1024),
        name="images",
    )(*map(keep, (blocks_used, subgrid_row, station_pair.T, visibilities, tracks, freq_ratio)))
    if direct:
        payloads = [sent[0]] + [shift_by(sent[shift], shift) for shift in range(1, owners)]
        payloads[0], screens[2] = lax.optimization_barrier((payloads[0], screens[2]))
        screens.append(flip(screens[2], 1))
        payloads[0], screens[1] = lax.optimization_barrier((payloads[0], screens[1]))
    else:
        by_owner = jnp.roll(sent[0], lax.axis_index("sub"), axis=0)
        payloads = [lax.all_to_all(by_owner, "sub", 0, 0, tiled=True)]
        screens = [lax.all_gather(aterm_screens, "sub", axis=1, tiled=True)]
    subgrids, stations, table = pl.pallas_call(
        subgrid_kernel,
        out_shape=[
            jax.ShapeDtypeStruct((base_count, 2, QROWS, LANES), jnp.float32),
            jax.ShapeDtypeStruct((groups, 8, LANES), jnp.int32),
            jax.ShapeDtypeStruct((LANES + 2 * SUB, 2 * LANES), jnp.float32),
        ],
        in_specs=[hbm] * 2 + [vmem] * len(payloads),
        out_specs=[vmem] * 3,
        scratch_shapes=[
            pltpu.SMEM((2, base_count), jnp.int32),
            pltpu.VMEM((ROWS, LANES), jnp.float32),
            pltpu.SemaphoreType.DMA((2,)),
        ],
        compiler_params=pltpu.CompilerParams(vmem_limit_bytes=48 * 1024 * 1024),
        cost_estimate=pl.CostEstimate(flops=30000000000, bytes_accessed=100000, transcendentals=0),
        name="subgrids",
    )(keep(subgrid_offsets.T), keep(tables()), *payloads)
    return pl.pallas_call(
        finish_kernel,
        out_shape=jax.ShapeDtypeStruct((1, base_count, 2, pixels), jnp.float32),
        in_specs=[vmem] * (3 + len(screens)),
        out_specs=vmem,
        scratch_shapes=[
            pltpu.VMEM((2 * SLOTS, 2 * QROWS, LANES), jnp.float32),
        ],
        compiler_params=pltpu.CompilerParams(vmem_limit_bytes=48 * 1024 * 1024),
        name="finish",
    )(table, stations, subgrids, *screens)


def solution(mesh):
    in_specs = (
        P("chan", ("grp", "sub"), None, None, None),
        P(("grp", "sub"), None, None),
        P(("grp", "chan"), None),
        P(("grp", "sub")),
        P(("grp", "sub")),
        P(("grp", "sub"), None),
        P(("grp", "sub"), None),
        P("chan", ("grp", "sub"), None, None),
    )
    out_specs = P("chan", ("grp", "sub"), None, None)
    return jax.shard_map(local, mesh=mesh, in_specs=in_specs, out_specs=out_specs, check_vma=False)
```

```python
import functools
import math

import jax
import jax.numpy as jnp
from jax import lax
from jax.experimental import pallas as pl
from jax.experimental.pallas import tpu as pltpu
from jax.sharding import PartitionSpec as P

SUB = 32
LANES = 128
SLOTS = LANES // SUB
QROWS = SUB // SLOTS
ROWS = 2 * SUB + 16
STEP = 8
HIGHEST = lax.Precision.HIGHEST
SINE = (3.14159027, -5.16740673, 2.54401052, -0.55946246)
COSINE = (0.99999325, -4.93393467, 4.0412481, -1.22203176)
SINE_LONG = (3.14159264, -5.16771008, 2.55007752, -0.59829129, 0.07765766)
COSINE_LONG = (0.99999995, -4.93479283, 4.05841135, -1.33187657, 0.21968961)


def series(terms, square):
    value = terms[-1]
    for term in terms[-2::-1]:
        value = term + square * value
    return value


def turn_cos_sin(turns, sine_terms=SINE_LONG, cosine_terms=COSINE_LONG):
    part = turns - jnp.round(turns)
    square = part * part
    sine = part * series(sine_terms, square)
    twice = sine + sine
    return 1.0 - twice * sine, twice * series(cosine_terms, square)


def times(a_real, a_imag, b_real, b_imag):
    return a_real * b_real - a_imag * b_imag, a_real * b_imag + a_imag * b_real


def iota(shape, axis):
    return lax.broadcasted_iota(jnp.int32, shape, axis)


def image_kernel(
    axis_size, used_hbm, row_hbm, pair_hbm, vis_hbm, tracks_hbm, freq_hbm, table_hbm, *rest
):
    send_refs, table_ref, scratch = rest[:-16], rest[-16], rest[-15:]
    (used_ref, row_ref, pair_ref, vis_ref, tracks_ref, freq_ref, lines_ref, turns_ref, powers_ref, total_ref,
     sems, wide_ref, image_ref, sums_ref, block_ref) = scratch
    base_count, blocks, _, samples = vis_ref.shape
    channels = freq_ref.shape[1]
    steps = samples // channels
    groups = -(-base_count // SLOTS)
    me = lax.axis_index("sub")
    lines = 2 * base_count
    tiles = samples // LANES
    sources = (
        (tracks_hbm, tracks_ref), (freq_hbm, freq_ref), (used_hbm, used_ref), (vis_hbm.at[0], vis_ref),
        (row_hbm, row_ref), (pair_hbm, pair_ref), (table_hbm, table_ref),
    )
    copies = [pltpu.make_async_copy(one, two, sems.at[n]) for n, (one, two) in enumerate(sources)]
    for copy in copies:
        copy.start()
    copies[0].wait()
    copies[1].wait()
    for b in range(base_count):
        lines_ref[2 * b : 2 * b + 2, :] = tracks_ref[b]
    wide_ref[...] = jnp.zeros_like(wide_ref)
    wide_ref[0:1, :channels] = freq_ref[...]
    wide = jnp.broadcast_to(wide_ref[0:1, :], (8, LANES))
    lane = iota((8, LANES), 1)
    ratio = jnp.concatenate(
        [jnp.take_along_axis(wide, (lane + m * LANES) // steps, axis=1) for m in range(tiles)], axis=1
    )[0:1] * (1.0 / SUB)
    weight = jnp.where(iota((lines, 1), 0) % 2 == 0, 1.0, float(QROWS))

    def prepare(j, _):
        moved = jnp.take_along_axis(lines_ref[...], iota((lines, LANES), 1) % steps + j * steps, axis=1)
        turns = jnp.concatenate([moved] * tiles, axis=1) * ratio
        turns = turns - jnp.round(turns)
        turns_ref[j] = turns
        one = turn_cos_sin(turns * weight, SINE, COSINE)
        two = times(*one, *one)
        for power, (real, imag) in enumerate((one, two)):
            powers_ref[j, 2 * power] = real
            powers_ref[j, 2 * power + 1] = imag
        return 0

    lax.fori_loop(0, blocks, prepare, 0, unroll=blocks if lines <= 8 else 1)
    total_ref[...] = jnp.zeros_like(total_ref)
    sums_ref[...] = jnp.zeros_like(sums_ref)
    q_start = (iota((QROWS, 1), 0) * SLOTS - SUB // 2).astype(jnp.float32)
    r_start = iota((QROWS, 1), 0).astype(jnp.float32) + 0.5
    for copy in copies[2:-1]:
        copy.wait()

    count = jnp.int32(0)
    for b in range(base_count):

        def note(j, _):
            block_ref[count + j] = b * blocks + j
            return 0

        lax.fori_loop(0, used_ref[b], note, 0)
        count = count + used_ref[b]
    for n in range(STEP - 1):
        block_ref[count + n] = 0

    def some_blocks(step, _):
        for n in range(STEP):
            block = block_ref[step * STEP + n]
            b, j = block // blocks, block % blocks
            sample = vis_ref[b, j].astype(jnp.float32)
            sample = jnp.where(step * STEP + n < count, sample, 0.0)

            def power(n, line):
                return powers_ref[j, 2 * n, pl.ds(line, 1), :], powers_ref[j, 2 * n + 1, pl.ds(line, 1), :]

            turns = [turns_ref[j, pl.ds(2 * b + axis, 1), :] for axis in range(2)]
            one = power(0, 2 * b)
            first = turn_cos_sin(turns[0] * q_start - turns[1] * 0.5, SINE, COSINE)
            first = times(*first, sample[0:1], sample[1:2])
            third = times(*first, *power(1, 2 * b))
            left = [first, times(*first, *one), third, times(*third, *one)]
            first = turn_cos_sin(turns[1] * r_start, SINE, COSINE)
            right = [first, times(*first, *power(0, 2 * b + 1))]
            left, right = (
                jnp.concatenate([pair[c] for c in range(2) for pair in pairs], axis=0).astype(jnp.bfloat16)
                for pairs in (left, right)
            )
            sums_ref[b] += lax.dot_general(left, right, (((1,), (1,)), ((), ())), preferred_element_type=jnp.float32)
        return 0

    lax.fori_loop(0, (count + STEP - 1) // STEP, some_blocks, 0)
    for b in range(base_count):
        image_ref[0 : 2 * SUB, 0:SUB] = sums_ref[b] * samples**-0.5
        stations = iota((ROWS - 2 * SUB, LANES), 0)
        stations = jnp.where(stations == 0, pair_ref[0, b], jnp.where(stations == 1, pair_ref[1, b], 0))
        image_ref[2 * SUB :, :] = stations.astype(jnp.float32)
        image = jnp.where(iota((ROWS, LANES), 1) < SUB, image_ref[...], 0.0)
        row = row_ref[b]
        owner = row // base_count
        slot = row % base_count
        place = lax.rem(owner - me + axis_size, axis_size)
        total_ref[place, slot // SLOTS] += pltpu.roll(image, (slot % SLOTS) * SUB, 1)
    if len(send_refs) > 1:
        for place, send_ref in enumerate(send_refs):
            send_ref[...] = total_ref[place].astype(jnp.bfloat16)
    else:
        send_refs[0][...] = total_ref[...].astype(jnp.bfloat16)
    copies[-1].wait()


def split_rows(value, rows_ref, first):
    for a in range(value.shape[1] // LANES):
        rows_ref[first + 2 * a : first + 2 * a + 2, :] = value[:, a * LANES : (a + 1) * LANES]


def swap(parts, lane):
    swapped = []
    for s in range(SLOTS):
        value = parts[s]
        for i in range(SLOTS):
            if i != s:
                value = jnp.where(lane // SUB == i, pltpu.roll(parts[i], ((i - s) % SLOTS) * SUB, 1), value)
        swapped.append(value)
    return swapped


def subgrid_kernel(offset_hbm, *rest):
    payload_refs, (pixels_ref, station_ref, offset_ref, rows_ref, sem) = rest[:-5], rest[-5:]
    copy = pltpu.make_async_copy(offset_hbm, offset_ref, sem)
    copy.start()
    lane = iota((QROWS, LANES), 1)
    q = iota((QROWS, LANES), 0) * SLOTS + lane // SUB - SUB // 2
    r = lane % SUB - SUB // 2
    line = lambda h: 1.0 - (2.0 * h.astype(jnp.float32) / (SUB + 2)) ** 2
    taper = line(q) * line(r)
    size = (LANES, LANES)
    column, pixel = iota(size, 0) % SUB, iota(size, 1) % SUB
    same = iota(size, 0) // SUB == iota(size, 1) // SUB
    above = same & (pixel - SUB // 2 == column % (SUB // 2))
    below = same & (SUB // 2 - 1 - pixel == column % (SUB // 2))
    even = jnp.where((above | below) & (column < SUB // 2), 1.0, 0.0)
    odd = jnp.where(column < SUB // 2, 0.0, jnp.where(below, 1.0, jnp.where(above, -1.0, 0.0)))
    unfold = jnp.concatenate([even, odd], axis=1).astype(jnp.bfloat16)
    for g in range(pixels_ref.shape[0] // SLOTS):
        parts = []
        for ref in payload_refs:
            parts += [ref[g]] if len(ref.shape) == 3 else [ref[p, g] for p in range(ref.shape[0])]
        whole = parts[0].astype(jnp.float32)
        for part in parts[1:]:
            whole = whole + part.astype(jnp.float32)
        rows_ref[...] = whole
        full = jnp.dot(whole[: 2 * SUB].astype(jnp.bfloat16), unfold, preferred_element_type=jnp.float32)
        real = full[:SUB, :LANES] + full[SUB:, LANES:]
        imag = full[SUB:, :LANES] - full[:SUB, LANES:]
        station_ref[g] = rows_ref[2 * SUB : 2 * SUB + 8, :].astype(jnp.int32)
        real = swap([real[i * QROWS : (i + 1) * QROWS] for i in range(SLOTS)], lane)
        imag = swap([imag[i * QROWS : (i + 1) * QROWS] for i in range(SLOTS)], lane)
        if g == 0:
            copy.wait()
        for s in range(SLOTS):
            slot = g * SLOTS + s
            turn = lax.rem(offset_ref[0, slot] * q + offset_ref[1, slot] * r, SUB)
            cosine, sine = turn_cos_sin(turn.astype(jnp.float32) * (1.0 / SUB))
            pixels_ref[slot, 0], pixels_ref[slot, 1] = times(real[s], imag[s], cosine * taper, -sine * taper)


def finish_kernel(table_ref, station_ref, pixels_ref, *rest):
    screens_refs, (out_ref, screen_ref) = rest[:-2], rest[-2:]
    me = lax.axis_index("sub")
    lane = iota((QROWS, LANES), 1)

    def screen(station):
        if len(screens_refs) == 1:
            return screens_refs[0][0, station]
        here = screens_refs[0].shape[1]
        away = me ^ (station // here)
        value = screens_refs[0][0, station % here]
        for flips in range(1, len(screens_refs)):
            value = jnp.where(away == flips, screens_refs[flips][0, station % here], value)
        return value

    for g in range(pixels_ref.shape[0] // SLOTS):
        weighted = []
        names = station_ref[g]
        for s in range(SLOTS):
            slot = g * SLOTS + s
            pair = []
            for e in range(2):
                n = 2 * s + e
                split_rows(screen(names[e, s * SUB]).astype(jnp.float32), screen_ref.at[n], 0)
                pair.append((screen_ref[n, pl.ds(0, QROWS, stride=2), :], screen_ref[n, pl.ds(1, QROWS, stride=2), :]))
            (p_real, p_imag), (s_real, s_imag) = pair
            gain = times(p_real, -p_imag, s_real, s_imag)
            weighted.append(times(pixels_ref[slot, 0], pixels_ref[slot, 1], *gain))
        planes = swap([pair[0] for pair in weighted], lane) + swap([pair[1] for pair in weighted], lane)
        planes = jnp.concatenate(planes, axis=0)
        half = jnp.dot(planes, table_ref[:LANES], precision=HIGHEST, preferred_element_type=jnp.float32)
        half_real = half[:SUB, :LANES] + half[SUB:, LANES:]
        half_imag = half[SUB:, :LANES] - half[:SUB, LANES:]
        half = jnp.concatenate([half_real, half_imag], axis=0)
        full = jnp.dot(table_ref[LANES:, : 2 * SUB], half, precision=HIGHEST, preferred_element_type=jnp.float32)
        for c in range(2):
            flat = swap([full[c * SUB + i * QROWS : c * SUB + (i + 1) * QROWS] for i in range(SLOTS)], lane)
            for s in range(SLOTS):
                for a in range(QROWS):
                    out_ref[0, g * SLOTS + s, c : c + 1, a * LANES : (a + 1) * LANES] = flat[s][a : a + 1]


def tables():
    h = [n - SUB // 2 for n in range(SUB)]
    order = [(n % QROWS) * SLOTS + n // QROWS - SUB // 2 for n in range(SUB)]
    turn = lambda f, x, y: f(2.0 * math.pi * ((x * y) % SUB) / SUB)
    r_table = [
        [turn(f, h[m % SUB], h[n % SUB]) if m // SUB == n // SUB else 0.0 for f in (math.cos, math.sin) for n in range(LANES)]
        for m in range(LANES)
    ]
    cos = [[turn(math.cos, x, y) / SUB for y in order] for x in order]
    sin = [[turn(math.sin, x, y) / SUB for y in order] for x in order]
    q_table = [c + s for c, s in zip(cos, sin)] + [[-v for v in s] + c for c, s in zip(cos, sin)]
    return jnp.array(r_table + [row + [0.0] * (2 * LANES - 2 * SUB) for row in q_table], jnp.float32)


def local(
    visibilities, tracks, freq_ratio, blocks_used, subgrid_row, station_pair, subgrid_offsets, aterm_screens
):
    owners = lax.axis_size("sub")
    base_count, blocks, _, samples = visibilities.shape[1:]
    groups = -(-base_count // SLOTS)
    here, _, pixels = aterm_screens.shape[1:]
    vmem = pl.BlockSpec(memory_space=pltpu.VMEM)
    hbm = pl.BlockSpec(memory_space=pltpu.HBM)
    keep = lambda x: pltpu.with_memory_space_constraint(x, pltpu.HBM)
    shift_by = lambda x, shift: lax.ppermute(x, "sub", [(n, (n + shift) % owners) for n in range(owners)])
    direct = owners == 4
    if direct:
        flip = lambda x, bits: lax.ppermute(x, "sub", [(n, n ^ bits) for n in range(owners)])
        screens = [aterm_screens, flip(aterm_screens, 1), flip(aterm_screens, 2)]
        sends = [jax.ShapeDtypeStruct((groups, ROWS, LANES), jnp.bfloat16)] * owners
    else:
        sends = [jax.ShapeDtypeStruct((owners, groups, ROWS, LANES), jnp.bfloat16)]
    sends.append(jax.ShapeDtypeStruct((LANES + 2 * SUB, 2 * LANES), jnp.float32))
    *sent, table = pl.pallas_call(
        functools.partial(image_kernel, owners),
        out_shape=sends,
        in_specs=[hbm] * 7,
        out_specs=[vmem] * len(sends),
        scratch_shapes=[
            pltpu.SMEM((base_count,), jnp.int32),
            pltpu.SMEM((base_count,), jnp.int32),
            pltpu.SMEM((2, base_count), jnp.int32),
            pltpu.VMEM(visibilities.shape[1:], jnp.bfloat16),
            pltpu.VMEM(tracks.shape, jnp.float32),
            pltpu.VMEM(freq_ratio.shape, jnp.float32),
            pltpu.VMEM((2 * base_count, tracks.shape[-1]), jnp.float32),
            pltpu.VMEM((blocks, 2 * base_count, samples), jnp.float32),
            pltpu.VMEM((blocks, 4, 2 * base_count, samples), jnp.float32),
            pltpu.VMEM((owners, groups, ROWS, LANES), jnp.float32),
            pltpu.SemaphoreType.DMA((7,)),
            pltpu.VMEM((8, LANES), jnp.float32),
            pltpu.VMEM((ROWS, LANES), jnp.float32),
            pltpu.VMEM((base_count, 2 * SUB, SUB), jnp.float32),
            pltpu.SMEM((base_count * blocks + STEP - 1,), jnp.int32),
        ],
        compiler_params=pltpu.CompilerParams(vmem_limit_bytes=48 * 1024 * 1024),
        name="images",
    )(*map(keep, (blocks_used, subgrid_row, station_pair.T, visibilities, tracks, freq_ratio, tables())))
    if direct:
        payloads = [sent[0]] + [shift_by(sent[shift], shift) for shift in (3,1,2)]
        payloads[0], screens[2] = lax.optimization_barrier((payloads[0], screens[2]))
        screens.append(flip(screens[2], 1))
        payloads[0], screens[1] = lax.optimization_barrier((payloads[0], screens[1]))
    else:
        by_owner = jnp.roll(sent[0], lax.axis_index("sub"), axis=0)
        payloads = [lax.all_to_all(by_owner, "sub", 0, 0, tiled=True)]
        screens = [lax.all_gather(aterm_screens, "sub", axis=1, tiled=True)]
    subgrids, stations = pl.pallas_call(
        subgrid_kernel,
        out_shape=[
            jax.ShapeDtypeStruct((base_count, 2, QROWS, LANES), jnp.float32),
            jax.ShapeDtypeStruct((groups, 8, LANES), jnp.int32),
        ],
        in_specs=[hbm] + [vmem] * len(payloads),
        out_specs=[vmem] * 2,
        scratch_shapes=[
            pltpu.SMEM((2, base_count), jnp.int32),
            pltpu.VMEM((ROWS, LANES), jnp.float32),
            pltpu.SemaphoreType.DMA(()),
        ],
        compiler_params=pltpu.CompilerParams(vmem_limit_bytes=48 * 1024 * 1024),
        cost_estimate=pl.CostEstimate(flops=30000000000, bytes_accessed=100000, transcendentals=0),
        name="subgrids",
    )(keep(subgrid_offsets.T), *payloads)
    return pl.pallas_call(
        finish_kernel,
        out_shape=jax.ShapeDtypeStruct((1, base_count, 2, pixels), jnp.float32),
        in_specs=[vmem] * (3 + len(screens)),
        out_specs=vmem,
        scratch_shapes=[
            pltpu.VMEM((2 * SLOTS, 2 * QROWS, LANES), jnp.float32),
        ],
        compiler_params=pltpu.CompilerParams(vmem_limit_bytes=48 * 1024 * 1024),
        name="finish",
    )(table, stations, subgrids, *screens)


def solution(mesh):
    in_specs = (
        P("chan", ("grp", "sub"), None, None, None),
        P(("grp", "sub"), None, None),
        P(("grp", "chan"), None),
        P(("grp", "sub")),
        P(("grp", "sub")),
        P(("grp", "sub"), None),
        P(("grp", "sub"), None),
        P("chan", ("grp", "sub"), None, None),
    )
    out_specs = P("chan", ("grp", "sub"), None, None)
    return jax.shard_map(local, mesh=mesh, in_specs=in_specs, out_specs=out_specs, check_vma=False)
```

```python
import functools
import math

import jax
import jax.numpy as jnp
import numpy as np
from jax import lax
from jax.experimental import pallas as pl
from jax.experimental.pallas import tpu as pltpu
from jax.sharding import PartitionSpec as P

SUB = 32
LANES = 128
SLOTS = LANES // SUB
QROWS = SUB // SLOTS
ROWS = 2 * SUB + 16
STEP = 16
SINE = (3.14159027, -5.16740673, 2.54401052, -0.55946246)
COSINE = (0.99999325, -4.93393467, 4.0412481, -1.22203176)
SINE_LONG = (3.14159264, -5.16771008, 2.55007752, -0.59829129, 0.07765766)
COSINE_LONG = (0.99999995, -4.93479283, 4.05841135, -1.33187657, 0.21968961)


def series(terms, square):
    value = terms[-1]
    for term in terms[-2::-1]:
        value = term + square * value
    return value


def turn_cos_sin(turns, sine_terms=SINE_LONG, cosine_terms=COSINE_LONG):
    part = turns - jnp.round(turns)
    square = part * part
    sine = part * series(sine_terms, square)
    twice = sine + sine
    return 1.0 - twice * sine, twice * series(cosine_terms, square)


def times(a_real, a_imag, b_real, b_imag):
    return a_real * b_real - a_imag * b_imag, a_real * b_imag + a_imag * b_real


def iota(shape, axis):
    return lax.broadcasted_iota(jnp.int32, shape, axis)


def pixel_lines():
    lane = iota((QROWS, LANES), 1)
    return iota((QROWS, LANES), 0) * SLOTS + lane // SUB - SUB // 2, lane % SUB - SUB // 2


def image_kernel(
    axis_size, used_hbm, row_hbm, pair_hbm, vis_hbm, tracks_hbm, freq_hbm, offset_hbm, table_hbm, *rest
):
    send_refs, (centre_ref, table_ref), scratch = rest[:-18], rest[-18:-16], rest[-16:]
    (used_ref, row_ref, pair_ref, vis_ref, tracks_ref, freq_ref, lines_ref, turns_ref, powers_ref, total_ref,
     sems, wide_ref, image_ref, sums_ref, block_ref, offset_ref) = scratch
    base_count, blocks, _, samples = vis_ref.shape
    channels = freq_ref.shape[1]
    steps = samples // channels
    groups = -(-base_count // SLOTS)
    me = lax.axis_index("sub")
    lines = 2 * base_count
    tiles = samples // LANES
    sources = (
        (tracks_hbm, tracks_ref), (freq_hbm, freq_ref), (used_hbm, used_ref), (vis_hbm.at[0], vis_ref),
        (row_hbm, row_ref), (pair_hbm, pair_ref), (offset_hbm, offset_ref),
        (table_hbm, table_ref),
    )
    copies = [pltpu.make_async_copy(one, two, sems.at[n]) for n, (one, two) in enumerate(sources)]
    for copy in copies:
        copy.start()
    copies[0].wait()
    copies[1].wait()
    for b in range(base_count):
        lines_ref[2 * b : 2 * b + 2, :] = tracks_ref[b]
    wide_ref[...] = jnp.zeros_like(wide_ref)
    wide_ref[0:1, :channels] = freq_ref[...]
    wide = jnp.broadcast_to(wide_ref[0:1, :], (8, LANES))
    lane = iota((8, LANES), 1)
    ratio = jnp.concatenate(
        [jnp.take_along_axis(wide, (lane + m * LANES) // steps, axis=1) for m in range(tiles)], axis=1
    )[0:1] * (1.0 / SUB)
    weight = jnp.where(iota((lines, 1), 0) % 2 == 0, 1.0, float(QROWS))

    def prepare(j, _):
        moved = jnp.take_along_axis(lines_ref[...], iota((lines, LANES), 1) % steps + j * steps, axis=1)
        turns = jnp.concatenate([moved] * tiles, axis=1) * ratio
        turns = turns - jnp.round(turns)
        turns_ref[j] = turns
        one = turn_cos_sin(turns * weight, SINE, COSINE)
        two = times(*one, *one)
        for power, (real, imag) in enumerate((one, two)):
            powers_ref[j, 2 * power] = real
            powers_ref[j, 2 * power + 1] = imag
        return 0

    lax.fori_loop(0, blocks, prepare, 0, unroll=blocks if lines <= 8 else 1)
    total_ref[...] = jnp.zeros_like(total_ref)
    sums_ref[...] = jnp.zeros_like(sums_ref)
    q_start = (iota((QROWS, 1), 0) * SLOTS - SUB // 2).astype(jnp.float32)
    r_start = iota((QROWS, 1), 0).astype(jnp.float32) + 0.5
    for copy in copies[2:-1]:
        copy.wait()

    q, r = pixel_lines()
    line = lambda h: 1.0 - (2.0 * h.astype(jnp.float32) / (SUB + 2)) ** 2
    taper = line(q) * line(r)
    for slot in range(base_count):
        turn = lax.rem(offset_ref[0, slot] * q + offset_ref[1, slot] * r, SUB)
        cosine, sine = turn_cos_sin(turn.astype(jnp.float32) * (1.0 / SUB))
        centre_ref[slot, 0] = cosine * taper
        centre_ref[slot, 1] = -sine * taper

    count = jnp.int32(0)
    for b in range(base_count):

        def note(j, _):
            block_ref[count + j] = b * blocks + j
            return 0

        lax.fori_loop(0, used_ref[b], note, 0)
        count = count + used_ref[b]
    for n in range(STEP - 1):
        block_ref[count + n] = 0

    def some_blocks(step, _):
        for n in range(STEP):
            block = block_ref[step * STEP + n]
            b, j = block // blocks, block % blocks
            sample = vis_ref[b, j].astype(jnp.float32)
            sample = jnp.where(step * STEP + n < count, sample, 0.0)

            def power(n, line):
                return powers_ref[j, 2 * n, pl.ds(line, 1), :], powers_ref[j, 2 * n + 1, pl.ds(line, 1), :]

            turns = [turns_ref[j, pl.ds(2 * b + axis, 1), :] for axis in range(2)]
            one = power(0, 2 * b)
            first = turn_cos_sin(turns[0] * q_start - turns[1] * 0.5, SINE, COSINE)
            first = times(*first, sample[0:1], sample[1:2])
            third = times(*first, *power(1, 2 * b))
            left = [first, times(*first, *one), third, times(*third, *one)]
            first = turn_cos_sin(turns[1] * r_start, SINE, COSINE)
            right = [first, times(*first, *power(0, 2 * b + 1))]
            left, right = (
                jnp.concatenate([pair[c] for c in range(2) for pair in pairs], axis=0).astype(jnp.bfloat16)
                for pairs in (left, right)
            )
            sums_ref[b] += lax.dot_general(left, right, (((1,), (1,)), ((), ())), preferred_element_type=jnp.float32)
        return 0

    lax.fori_loop(0, (count + STEP - 1) // STEP, some_blocks, 0)
    for b in range(base_count):
        image_ref[0 : 2 * SUB, 0:SUB] = sums_ref[b] * samples**-0.5
        stations = iota((ROWS - 2 * SUB, LANES), 0)
        stations = jnp.where(stations == 0, pair_ref[0, b], jnp.where(stations == 1, pair_ref[1, b], 0))
        image_ref[2 * SUB :, :] = stations.astype(jnp.float32)
        image = jnp.where(iota((ROWS, LANES), 1) < SUB, image_ref[...], 0.0)
        row = row_ref[b]
        owner = row // base_count
        slot = row % base_count
        place = lax.rem(owner - me + axis_size, axis_size)
        total_ref[place, slot // SLOTS] += pltpu.roll(image, (slot % SLOTS) * SUB, 1)
    if len(send_refs) > 1:
        for place, send_ref in enumerate(send_refs):
            send_ref[...] = total_ref[place].astype(jnp.bfloat16)
    else:
        send_refs[0][...] = total_ref[...].astype(jnp.bfloat16)
    copies[-1].wait()


def split_rows(value, rows_ref, first):
    for a in range(value.shape[1] // LANES):
        rows_ref[first + 2 * a : first + 2 * a + 2, :] = value[:, a * LANES : (a + 1) * LANES]


def halves(value):
    high = value.astype(jnp.bfloat16)
    return high, (value - high.astype(jnp.float32)).astype(jnp.bfloat16)


def swap(parts, lane):
    swapped = []
    for s in range(SLOTS):
        value = parts[s]
        for i in range(SLOTS):
            if i != s:
                value = jnp.where(lane // SUB == i, pltpu.roll(parts[i], ((i - s) % SLOTS) * SUB, 1), value)
        swapped.append(value)
    return swapped


def subgrid_kernel(centre_ref, *rest):
    payload_refs, (pixels_ref, station_ref) = rest[:-2], rest[-2:]
    lane = iota((QROWS, LANES), 1)
    size = (LANES, LANES)
    column, pixel = iota(size, 0) % SUB, iota(size, 1) % SUB
    same = iota(size, 0) // SUB == iota(size, 1) // SUB
    above = same & (pixel - SUB // 2 == column % (SUB // 2))
    below = same & (SUB // 2 - 1 - pixel == column % (SUB // 2))
    even = jnp.where((above | below) & (column < SUB // 2), 1.0, 0.0)
    odd = jnp.where(column < SUB // 2, 0.0, jnp.where(below, 1.0, jnp.where(above, -1.0, 0.0)))
    unfold = jnp.concatenate([even, odd], axis=1).astype(jnp.bfloat16)
    for g in range(pixels_ref.shape[0] // SLOTS):
        parts = []
        for ref in payload_refs:
            parts += [ref[g]] if len(ref.shape) == 3 else [ref[p, g] for p in range(ref.shape[0])]
        whole = parts[0].astype(jnp.float32)
        for part in parts[1:]:
            whole = whole + part.astype(jnp.float32)
        full = jnp.dot(whole[: 2 * SUB].astype(jnp.bfloat16), unfold, preferred_element_type=jnp.float32)
        real = full[:SUB, :LANES] + full[SUB:, LANES:]
        imag = full[SUB:, :LANES] - full[:SUB, LANES:]
        station_ref[g] = whole[2 * SUB : 2 * SUB + 8].astype(jnp.int32)
        real = swap([real[i * QROWS : (i + 1) * QROWS] for i in range(SLOTS)], lane)
        imag = swap([imag[i * QROWS : (i + 1) * QROWS] for i in range(SLOTS)], lane)
        for s in range(SLOTS):
            slot = g * SLOTS + s
            pixels_ref[slot, 0], pixels_ref[slot, 1] = times(real[s], imag[s], centre_ref[slot, 0], centre_ref[slot, 1])


def finish_kernel(table_ref, station_ref, pixels_ref, *rest):
    screens_refs, (out_ref, screen_ref) = rest[:-2], rest[-2:]
    second = table_ref.shape[0] // 2
    me = lax.axis_index("sub")
    lane = iota((QROWS, LANES), 1)

    def screen(station):
        if len(screens_refs) == 1:
            return screens_refs[0][0, station]
        here = screens_refs[0].shape[1]
        away = me ^ (station // here)
        value = screens_refs[0][0, station % here]
        for flips in range(1, len(screens_refs)):
            value = jnp.where(away == flips, screens_refs[flips][0, station % here], value)
        return value

    for g in range(pixels_ref.shape[0] // SLOTS):
        weighted = []
        names = station_ref[g]
        for s in range(SLOTS):
            slot = g * SLOTS + s
            pair = []
            for e in range(2):
                n = 2 * s + e
                split_rows(screen(names[e, s * SUB]).astype(jnp.float32), screen_ref.at[n], 0)
                pair.append((screen_ref[n, pl.ds(0, QROWS, stride=2), :], screen_ref[n, pl.ds(1, QROWS, stride=2), :]))
            (p_real, p_imag), (s_real, s_imag) = pair
            gain = times(p_real, -p_imag, s_real, s_imag)
            weighted.append(times(pixels_ref[slot, 0], pixels_ref[slot, 1], *gain))
        planes = swap([pair[0] for pair in weighted], lane) + swap([pair[1] for pair in weighted], lane)
        planes = jnp.concatenate(planes, axis=0)
        high, low = halves(planes)
        wide = jnp.dot(jnp.concatenate([high, low], axis=0), table_ref[:LANES], preferred_element_type=jnp.float32)
        half = wide[: 2 * SUB] + wide[2 * SUB :]
        half = half + jnp.dot(high, table_ref[second : second + LANES], preferred_element_type=jnp.float32)
        half_real = half[:SUB, :LANES] + half[SUB:, LANES:]
        half_imag = half[SUB:, :LANES] - half[:SUB, LANES:]
        half = jnp.concatenate([half_real, half_imag], axis=0)
        high, low = halves(half)
        q_high = table_ref[LANES:second, : 2 * SUB]
        q_low = table_ref[second + LANES :, : 2 * SUB]
        wide = jnp.dot(q_high, jnp.concatenate([high, low], axis=1), preferred_element_type=jnp.float32)
        full = wide[:, :LANES] + wide[:, LANES:] + jnp.dot(q_low, high, preferred_element_type=jnp.float32)
        for c in range(2):
            flat = swap([full[c * SUB + i * QROWS : c * SUB + (i + 1) * QROWS] for i in range(SLOTS)], lane)
            for s in range(SLOTS):
                for a in range(QROWS):
                    out_ref[0, g * SLOTS + s, c : c + 1, a * LANES : (a + 1) * LANES] = flat[s][a : a + 1]


def tables():
    h = [n - SUB // 2 for n in range(SUB)]
    order = [(n % QROWS) * SLOTS + n // QROWS - SUB // 2 for n in range(SUB)]
    turn = lambda f, x, y: f(2.0 * math.pi * ((x * y) % SUB) / SUB)
    r_table = [
        [turn(f, h[m % SUB], h[n % SUB]) if m // SUB == n // SUB else 0.0 for f in (math.cos, math.sin) for n in range(LANES)]
        for m in range(LANES)
    ]
    cos = [[turn(math.cos, x, y) / SUB for y in order] for x in order]
    sin = [[turn(math.sin, x, y) / SUB for y in order] for x in order]
    q_table = [c + s for c, s in zip(cos, sin)] + [[-v for v in s] + c for c, s in zip(cos, sin)]
    table = np.array(r_table + [row + [0.0] * (2 * LANES - 2 * SUB) for row in q_table], np.float32)
    high = table.astype(jnp.bfloat16)
    return jnp.array(np.concatenate([high, (table - high.astype(np.float32)).astype(jnp.bfloat16)], axis=0))


def local(
    visibilities, tracks, freq_ratio, blocks_used, subgrid_row, station_pair, subgrid_offsets, aterm_screens
):
    owners = lax.axis_size("sub")
    base_count, blocks, _, samples = visibilities.shape[1:]
    groups = -(-base_count // SLOTS)
    here, _, pixels = aterm_screens.shape[1:]
    vmem = pl.BlockSpec(memory_space=pltpu.VMEM)
    hbm = pl.BlockSpec(memory_space=pltpu.HBM)
    keep = lambda x: pltpu.with_memory_space_constraint(x, pltpu.HBM)
    shift_by = lambda x, shift: lax.ppermute(x, "sub", [(n, (n + shift) % owners) for n in range(owners)])
    direct = owners == 4
    if direct:
        flip = lambda x, bits: lax.ppermute(x, "sub", [(n, n ^ bits) for n in range(owners)])
        screens = [aterm_screens, flip(aterm_screens, 1), flip(aterm_screens, 2)]
        sends = [jax.ShapeDtypeStruct((groups, ROWS, LANES), jnp.bfloat16)] * owners
    else:
        sends = [jax.ShapeDtypeStruct((owners, groups, ROWS, LANES), jnp.bfloat16)]
    sends.append(jax.ShapeDtypeStruct((base_count, 2, QROWS, LANES), jnp.float32))
    sends.append(jax.ShapeDtypeStruct((2 * (LANES + 2 * SUB), 2 * LANES), jnp.bfloat16))
    *sent, centre, table = pl.pallas_call(
        functools.partial(image_kernel, owners),
        out_shape=sends,
        in_specs=[hbm] * 8,
        out_specs=[vmem] * len(sends),
        scratch_shapes=[
            pltpu.SMEM((base_count,), jnp.int32),
            pltpu.SMEM((base_count,), jnp.int32),
            pltpu.SMEM((2, base_count), jnp.int32),
            pltpu.VMEM(visibilities.shape[1:], jnp.bfloat16),
            pltpu.VMEM(tracks.shape, jnp.float32),
            pltpu.VMEM(freq_ratio.shape, jnp.float32),
            pltpu.VMEM((2 * base_count, tracks.shape[-1]), jnp.float32),
            pltpu.VMEM((blocks, 2 * base_count, samples), jnp.float32),
            pltpu.VMEM((blocks, 4, 2 * base_count, samples), jnp.float32),
            pltpu.VMEM((owners, groups, ROWS, LANES), jnp.float32),
            pltpu.SemaphoreType.DMA((8,)),
            pltpu.VMEM((8, LANES), jnp.float32),
            pltpu.VMEM((ROWS, LANES), jnp.float32),
            pltpu.VMEM((base_count, 2 * SUB, SUB), jnp.float32),
            pltpu.SMEM((base_count * blocks + STEP - 1,), jnp.int32),
            pltpu.SMEM((2, base_count), jnp.int32),
        ],
        compiler_params=pltpu.CompilerParams(vmem_limit_bytes=48 * 1024 * 1024),
        name="images",
    )(*map(keep, (blocks_used, subgrid_row, station_pair.T, visibilities, tracks, freq_ratio, subgrid_offsets.T, tables())))
    if direct:
        payloads = [sent[0]] + [shift_by(sent[shift], shift) for shift in (3, 1, 2)]
        payloads[0], screens[2] = lax.optimization_barrier((payloads[0], screens[2]))
        screens.append(flip(screens[2], 1))
        payloads[0], screens[1] = lax.optimization_barrier((payloads[0], screens[1]))
    else:
        by_owner = jnp.roll(sent[0], lax.axis_index("sub"), axis=0)
        payloads = [lax.all_to_all(by_owner, "sub", 0, 0, tiled=True)]
        screens = [lax.all_gather(aterm_screens, "sub", axis=1, tiled=True)]
    subgrids, stations = pl.pallas_call(
        subgrid_kernel,
        out_shape=[
            jax.ShapeDtypeStruct((base_count, 2, QROWS, LANES), jnp.float32),
            jax.ShapeDtypeStruct((groups, 8, LANES), jnp.int32),
        ],
        in_specs=[vmem] * (1 + len(payloads)),
        out_specs=[vmem] * 2,
        compiler_params=pltpu.CompilerParams(vmem_limit_bytes=48 * 1024 * 1024),
        cost_estimate=pl.CostEstimate(flops=10000000000, bytes_accessed=100000, transcendentals=0),
        name="subgrids",
    )(centre, *payloads)
    return pl.pallas_call(
        finish_kernel,
        out_shape=jax.ShapeDtypeStruct((1, base_count, 2, pixels), jnp.float32),
        in_specs=[vmem] * (3 + len(screens)),
        out_specs=vmem,
        scratch_shapes=[
            pltpu.VMEM((2 * SLOTS, 2 * QROWS, LANES), jnp.float32),
        ],
        compiler_params=pltpu.CompilerParams(vmem_limit_bytes=48 * 1024 * 1024),
        name="finish",
    )(table, stations, subgrids, *screens)


def solution(mesh):
    in_specs = (
        P("chan", ("grp", "sub"), None, None, None),
        P(("grp", "sub"), None, None),
        P(("grp", "chan"), None),
        P(("grp", "sub")),
        P(("grp", "sub")),
        P(("grp", "sub"), None),
        P(("grp", "sub"), None),
        P("chan", ("grp", "sub"), None, None),
    )
    out_specs = P("chan", ("grp", "sub"), None, None)
    return jax.shard_map(local, mesh=mesh, in_specs=in_specs, out_specs=out_specs, check_vma=False)
```

```python
import functools
import math

import jax
import jax.numpy as jnp
import numpy as np
from jax import lax
from jax.experimental import pallas as pl
from jax.experimental.pallas import tpu as pltpu
from jax.sharding import PartitionSpec as P

SUB = 32
LANES = 128
SLOTS = LANES // SUB
QROWS = SUB // SLOTS
ROWS = 2 * SUB + 16
STEP = 16
SINE = (3.14159027, -5.16740673, 2.54401052, -0.55946246)
COSINE = (0.99999325, -4.93393467, 4.0412481, -1.22203176)
SINE_LONG = (3.14159264, -5.16771008, 2.55007752, -0.59829129, 0.07765766)
COSINE_LONG = (0.99999995, -4.93479283, 4.05841135, -1.33187657, 0.21968961)


def series(terms, square):
    value = terms[-1]
    for term in terms[-2::-1]:
        value = term + square * value
    return value


def turn_cos_sin(turns, sine_terms=SINE_LONG, cosine_terms=COSINE_LONG):
    part = turns - jnp.round(turns)
    square = part * part
    sine = part * series(sine_terms, square)
    twice = sine + sine
    return 1.0 - twice * sine, twice * series(cosine_terms, square)


def times(a_real, a_imag, b_real, b_imag):
    return a_real * b_real - a_imag * b_imag, a_real * b_imag + a_imag * b_real


def iota(shape, axis):
    return lax.broadcasted_iota(jnp.int32, shape, axis)


def pixel_lines():
    lane = iota((QROWS, LANES), 1)
    return iota((QROWS, LANES), 0) * SLOTS + lane // SUB - SUB // 2, lane % SUB - SUB // 2


def image_kernel(
    axis_size, used_hbm, row_hbm, pair_hbm, vis_hbm, tracks_hbm, freq_hbm, offset_hbm, table_hbm, *rest
):
    send_refs, (centre_ref, table_ref), scratch = rest[:-18], rest[-18:-16], rest[-16:]
    (used_ref, row_ref, pair_ref, vis_ref, tracks_ref, freq_ref, lines_ref, turns_ref, powers_ref, total_ref,
     sems, wide_ref, image_ref, sums_ref, block_ref, offset_ref) = scratch
    base_count, blocks, _, samples = vis_ref.shape
    channels = freq_ref.shape[1]
    steps = samples // channels
    groups = -(-base_count // SLOTS)
    me = lax.axis_index("sub")
    lines = 2 * base_count
    tiles = samples // LANES
    sources = (
        (tracks_hbm, tracks_ref), (freq_hbm, freq_ref), (used_hbm, used_ref), (vis_hbm.at[0], vis_ref),
        (row_hbm, row_ref), (pair_hbm, pair_ref), (offset_hbm, offset_ref),
        (table_hbm, table_ref),
    )
    copies = [pltpu.make_async_copy(one, two, sems.at[n]) for n, (one, two) in enumerate(sources)]
    for copy in copies:
        copy.start()
    copies[0].wait()
    copies[1].wait()
    for b in range(base_count):
        lines_ref[2 * b : 2 * b + 2, :] = tracks_ref[b]
    wide_ref[...] = jnp.zeros_like(wide_ref)
    wide_ref[0:1, :channels] = freq_ref[...]
    wide = jnp.broadcast_to(wide_ref[0:1, :], (8, LANES))
    lane = iota((8, LANES), 1)
    ratio = jnp.concatenate(
        [jnp.take_along_axis(wide, (lane + m * LANES) // steps, axis=1) for m in range(tiles)], axis=1
    )[0:1] * (1.0 / SUB)
    weight = jnp.where(iota((lines, 1), 0) % 2 == 0, 1.0, float(QROWS))

    def prepare(j, _):
        moved = jnp.take_along_axis(lines_ref[...], iota((lines, LANES), 1) % steps + j * steps, axis=1)
        turns = jnp.concatenate([moved] * tiles, axis=1) * ratio
        turns = turns - jnp.round(turns)
        turns_ref[j] = turns
        one = turn_cos_sin(turns * weight, SINE, COSINE)
        two = times(*one, *one)
        for power, (real, imag) in enumerate((one, two)):
            powers_ref[j, 2 * power] = real
            powers_ref[j, 2 * power + 1] = imag
        return 0

    lax.fori_loop(0, blocks, prepare, 0, unroll=blocks if lines <= 8 else 1)
    total_ref[...] = jnp.zeros_like(total_ref)
    sums_ref[...] = jnp.zeros_like(sums_ref)
    q_start = (iota((QROWS, 1), 0) * SLOTS - SUB // 2).astype(jnp.float32)
    r_start = iota((QROWS, 1), 0).astype(jnp.float32) + 0.5
    for copy in copies[2:-1]:
        copy.wait()

    q, r = pixel_lines()
    line = lambda h: 1.0 - (2.0 * h.astype(jnp.float32) / (SUB + 2)) ** 2
    taper = line(q) * line(r)
    for slot in range(base_count):
        turn = lax.rem(offset_ref[0, slot] * q + offset_ref[1, slot] * r, SUB)
        cosine, sine = turn_cos_sin(turn.astype(jnp.float32) * (1.0 / SUB))
        centre_ref[slot, 0] = cosine * taper
        centre_ref[slot, 1] = -sine * taper

    count = jnp.int32(0)
    for b in range(base_count):

        def note(j, _):
            block_ref[count + j] = b * blocks + j
            return 0

        lax.fori_loop(0, used_ref[b], note, 0)
        count = count + used_ref[b]
    for n in range(STEP - 1):
        block_ref[count + n] = 0

    def some_blocks(step, _):
        for n in range(STEP):
            block = block_ref[step * STEP + n]
            b, j = block // blocks, block % blocks
            sample = vis_ref[b, j].astype(jnp.float32)
            sample = jnp.where(step * STEP + n < count, sample, 0.0)

            def power(n, line):
                return powers_ref[j, 2 * n, pl.ds(line, 1), :], powers_ref[j, 2 * n + 1, pl.ds(line, 1), :]

            turns = [turns_ref[j, pl.ds(2 * b + axis, 1), :] for axis in range(2)]
            one = power(0, 2 * b)
            first = turn_cos_sin(turns[0] * q_start - turns[1] * 0.5, SINE, COSINE)
            first = times(*first, sample[0:1], sample[1:2])
            third = times(*first, *power(1, 2 * b))
            left = [first, times(*first, *one), third, times(*third, *one)]
            first = turn_cos_sin(turns[1] * r_start, SINE, COSINE)
            right = [first, times(*first, *power(0, 2 * b + 1))]
            left, right = (
                jnp.concatenate([pair[c] for c in range(2) for pair in pairs], axis=0).astype(jnp.bfloat16)
                for pairs in (left, right)
            )
            sums_ref[b] += lax.dot_general(left, right, (((1,), (1,)), ((), ())), preferred_element_type=jnp.float32)
        return 0

    lax.fori_loop(0, (count + STEP - 1) // STEP, some_blocks, 0)
    for b in range(base_count):
        image_ref[0 : 2 * SUB, 0:SUB] = sums_ref[b] * samples**-0.5
        stations = iota((ROWS - 2 * SUB, LANES), 0)
        stations = jnp.where(stations == 0, pair_ref[0, b], jnp.where(stations == 1, pair_ref[1, b], 0))
        image_ref[2 * SUB :, :] = stations.astype(jnp.float32)
        image = jnp.where(iota((ROWS, LANES), 1) < SUB, image_ref[...], 0.0)
        row = row_ref[b]
        owner = row // base_count
        slot = row % base_count
        place = lax.rem(owner - me + axis_size, axis_size)
        total_ref[place, slot // SLOTS] += pltpu.roll(image, (slot % SLOTS) * SUB, 1)
    if len(send_refs) > 1:
        for place, send_ref in enumerate(send_refs):
            send_ref[...] = total_ref[place].astype(jnp.bfloat16)
    else:
        send_refs[0][...] = total_ref[...].astype(jnp.bfloat16)
    copies[-1].wait()


def split_rows(value, rows_ref, first):
    for a in range(value.shape[1] // LANES):
        rows_ref[first + 2 * a : first + 2 * a + 2, :] = value[:, a * LANES : (a + 1) * LANES]


def halves(value):
    high = value.astype(jnp.bfloat16)
    return high, (value - high.astype(jnp.float32)).astype(jnp.bfloat16)


def swap(parts, lane):
    swapped = []
    for s in range(SLOTS):
        value = parts[s]
        for i in range(SLOTS):
            if i != s:
                value = jnp.where(lane // SUB == i, pltpu.roll(parts[i], ((i - s) % SLOTS) * SUB, 1), value)
        swapped.append(value)
    return swapped


def subgrid_kernel(centre_ref, *rest):
    payload_refs, (pixels_ref, station_ref) = rest[:-2], rest[-2:]
    lane = iota((QROWS, LANES), 1)
    size = (LANES, LANES)
    column, pixel = iota(size, 0) % SUB, iota(size, 1) % SUB
    same = iota(size, 0) // SUB == iota(size, 1) // SUB
    above = same & (pixel - SUB // 2 == column % (SUB // 2))
    below = same & (SUB // 2 - 1 - pixel == column % (SUB // 2))
    even = jnp.where((above | below) & (column < SUB // 2), 1.0, 0.0)
    odd = jnp.where(column < SUB // 2, 0.0, jnp.where(below, 1.0, jnp.where(above, -1.0, 0.0)))
    unfold = jnp.concatenate([even, odd], axis=1).astype(jnp.bfloat16)
    for g in range(pixels_ref.shape[0] // SLOTS):
        parts = []
        for ref in payload_refs:
            parts += [ref[g]] if len(ref.shape) == 3 else [ref[p, g] for p in range(ref.shape[0])]
        whole = parts[0].astype(jnp.float32)
        for part in parts[1:]:
            whole = whole + part.astype(jnp.float32)
        full = jnp.dot(whole[: 2 * SUB].astype(jnp.bfloat16), unfold, preferred_element_type=jnp.float32)
        real = full[:SUB, :LANES] + full[SUB:, LANES:]
        imag = full[SUB:, :LANES] - full[:SUB, LANES:]
        station_ref[g] = whole[2 * SUB : 2 * SUB + 8].astype(jnp.int32)
        real = swap([real[i * QROWS : (i + 1) * QROWS] for i in range(SLOTS)], lane)
        imag = swap([imag[i * QROWS : (i + 1) * QROWS] for i in range(SLOTS)], lane)
        for s in range(SLOTS):
            slot = g * SLOTS + s
            pixels_ref[slot, 0], pixels_ref[slot, 1] = times(real[s], imag[s], centre_ref[slot, 0], centre_ref[slot, 1])


def finish_kernel(table_ref, station_ref, pixels_ref, *rest):
    screens_refs, (out_ref, screen_ref) = rest[:-2], rest[-2:]
    second = table_ref.shape[0] // 2
    me = lax.axis_index("sub")
    lane = iota((QROWS, LANES), 1)

    def screen(station):
        if len(screens_refs) == 1:
            return screens_refs[0][0, station]
        here = screens_refs[0].shape[1]
        away = me ^ (station // here)
        value = screens_refs[0][0, station % here].astype(jnp.float32)
        for flips in range(1, len(screens_refs)):
            value = jnp.where(away == flips, screens_refs[flips][0, station % here].astype(jnp.float32), value)
        return value

    for g in range(pixels_ref.shape[0] // SLOTS):
        weighted = []
        names = station_ref[g]
        for s in range(SLOTS):
            slot = g * SLOTS + s
            pair = []
            for e in range(2):
                n = 2 * s + e
                split_rows(screen(names[e, s * SUB]).astype(jnp.float32), screen_ref.at[n], 0)
                pair.append((screen_ref[n, pl.ds(0, QROWS, stride=2), :], screen_ref[n, pl.ds(1, QROWS, stride=2), :]))
            (p_real, p_imag), (s_real, s_imag) = pair
            gain = times(p_real, -p_imag, s_real, s_imag)
            weighted.append(times(pixels_ref[slot, 0], pixels_ref[slot, 1], *gain))
        planes = swap([pair[0] for pair in weighted], lane) + swap([pair[1] for pair in weighted], lane)
        planes = jnp.concatenate(planes, axis=0)
        high, low = halves(planes)
        wide = jnp.dot(jnp.concatenate([high, low], axis=0), table_ref[:LANES], preferred_element_type=jnp.float32)
        half = wide[: 2 * SUB] + wide[2 * SUB :]
        half = half + jnp.dot(high, table_ref[second : second + LANES], preferred_element_type=jnp.float32)
        half_real = half[:SUB, :LANES] + half[SUB:, LANES:]
        half_imag = half[SUB:, :LANES] - half[:SUB, LANES:]
        half = jnp.concatenate([half_real, half_imag], axis=0)
        high, low = halves(half)
        q_high = table_ref[LANES:second, : 2 * SUB]
        q_low = table_ref[second + LANES :, : 2 * SUB]
        wide = jnp.dot(q_high, jnp.concatenate([high, low], axis=1), preferred_element_type=jnp.float32)
        full = wide[:, :LANES] + wide[:, LANES:] + jnp.dot(q_low, high, preferred_element_type=jnp.float32)
        for c in range(2):
            flat = swap([full[c * SUB + i * QROWS : c * SUB + (i + 1) * QROWS] for i in range(SLOTS)], lane)
            for s in range(SLOTS):
                for a in range(QROWS):
                    out_ref[0, g * SLOTS + s, c : c + 1, a * LANES : (a + 1) * LANES] = flat[s][a : a + 1]


def tables():
    h = [n - SUB // 2 for n in range(SUB)]
    order = [(n % QROWS) * SLOTS + n // QROWS - SUB // 2 for n in range(SUB)]
    turn = lambda f, x, y: f(2.0 * math.pi * ((x * y) % SUB) / SUB)
    r_table = [
        [turn(f, h[m % SUB], h[n % SUB]) if m // SUB == n // SUB else 0.0 for f in (math.cos, math.sin) for n in range(LANES)]
        for m in range(LANES)
    ]
    cos = [[turn(math.cos, x, y) / SUB for y in order] for x in order]
    sin = [[turn(math.sin, x, y) / SUB for y in order] for x in order]
    q_table = [c + s for c, s in zip(cos, sin)] + [[-v for v in s] + c for c, s in zip(cos, sin)]
    table = np.array(r_table + [row + [0.0] * (2 * LANES - 2 * SUB) for row in q_table], np.float32)
    high = table.astype(jnp.bfloat16)
    return jnp.array(np.concatenate([high, (table - high.astype(np.float32)).astype(jnp.bfloat16)], axis=0))


def local(
    visibilities, tracks, freq_ratio, blocks_used, subgrid_row, station_pair, subgrid_offsets, aterm_screens
):
    owners = lax.axis_size("sub")
    base_count, blocks, _, samples = visibilities.shape[1:]
    groups = -(-base_count // SLOTS)
    here, _, pixels = aterm_screens.shape[1:]
    vmem = pl.BlockSpec(memory_space=pltpu.VMEM)
    hbm = pl.BlockSpec(memory_space=pltpu.HBM)
    keep = lambda x: pltpu.with_memory_space_constraint(x, pltpu.HBM)
    shift_by = lambda x, shift: lax.ppermute(x, "sub", [(n, (n + shift) % owners) for n in range(owners)])
    direct = owners == 4
    if direct:
        flip = lambda x, bits: lax.ppermute(x, "sub", [(n, n ^ bits) for n in range(owners)])
        screens = [aterm_screens, flip(aterm_screens, 1), flip(aterm_screens, 2)]
        sends = [jax.ShapeDtypeStruct((groups, ROWS, LANES), jnp.bfloat16)] * owners
    else:
        sends = [jax.ShapeDtypeStruct((owners, groups, ROWS, LANES), jnp.bfloat16)]
    sends.append(jax.ShapeDtypeStruct((base_count, 2, QROWS, LANES), jnp.float32))
    sends.append(jax.ShapeDtypeStruct((2 * (LANES + 2 * SUB), 2 * LANES), jnp.bfloat16))
    *sent, centre, table = pl.pallas_call(
        functools.partial(image_kernel, owners),
        out_shape=sends,
        in_specs=[hbm] * 8,
        out_specs=[vmem] * len(sends),
        scratch_shapes=[
            pltpu.SMEM((base_count,), jnp.int32),
            pltpu.SMEM((base_count,), jnp.int32),
            pltpu.SMEM((2, base_count), jnp.int32),
            pltpu.VMEM(visibilities.shape[1:], jnp.bfloat16),
            pltpu.VMEM(tracks.shape, jnp.float32),
            pltpu.VMEM(freq_ratio.shape, jnp.float32),
            pltpu.VMEM((2 * base_count, tracks.shape[-1]), jnp.float32),
            pltpu.VMEM((blocks, 2 * base_count, samples), jnp.float32),
            pltpu.VMEM((blocks, 4, 2 * base_count, samples), jnp.float32),
            pltpu.VMEM((owners, groups, ROWS, LANES), jnp.float32),
            pltpu.SemaphoreType.DMA((8,)),
            pltpu.VMEM((8, LANES), jnp.float32),
            pltpu.VMEM((ROWS, LANES), jnp.float32),
            pltpu.VMEM((base_count, 2 * SUB, SUB), jnp.float32),
            pltpu.SMEM((base_count * blocks + STEP - 1,), jnp.int32),
            pltpu.SMEM((2, base_count), jnp.int32),
        ],
        compiler_params=pltpu.CompilerParams(vmem_limit_bytes=48 * 1024 * 1024),
        name="images",
    )(*map(keep, (blocks_used, subgrid_row, station_pair.T, visibilities, tracks, freq_ratio, subgrid_offsets.T, tables())))
    if direct:
        payloads = [sent[0]] + [shift_by(sent[shift], shift) for shift in (3, 1, 2)]
        payloads[0], screens[2] = lax.optimization_barrier((payloads[0], screens[2]))
        screens.append(flip(screens[2], 1))
        payloads[0], screens[1] = lax.optimization_barrier((payloads[0], screens[1]))
    else:
        by_owner = jnp.roll(sent[0], lax.axis_index("sub"), axis=0)
        payloads = [lax.all_to_all(by_owner, "sub", 0, 0, tiled=True)]
        screens = [lax.all_gather(aterm_screens, "sub", axis=1, tiled=True)]
    subgrids, stations = pl.pallas_call(
        subgrid_kernel,
        out_shape=[
            jax.ShapeDtypeStruct((base_count, 2, QROWS, LANES), jnp.float32),
            jax.ShapeDtypeStruct((groups, 8, LANES), jnp.int32),
        ],
        in_specs=[vmem] * (1 + len(payloads)),
        out_specs=[vmem] * 2,
        compiler_params=pltpu.CompilerParams(vmem_limit_bytes=48 * 1024 * 1024),
        cost_estimate=pl.CostEstimate(flops=10000000000, bytes_accessed=100000, transcendentals=0),
        name="subgrids",
    )(centre, *payloads)
    return pl.pallas_call(
        finish_kernel,
        out_shape=jax.ShapeDtypeStruct((1, base_count, 2, pixels), jnp.float32),
        in_specs=[vmem] * (3 + len(screens)),
        out_specs=vmem,
        scratch_shapes=[
            pltpu.VMEM((2 * SLOTS, 2 * QROWS, LANES), jnp.float32),
        ],
        compiler_params=pltpu.CompilerParams(vmem_limit_bytes=48 * 1024 * 1024),
        name="finish",
    )(table, stations, subgrids, *screens)


def solution(mesh):
    in_specs = (
        P("chan", ("grp", "sub"), None, None, None),
        P(("grp", "sub"), None, None),
        P(("grp", "chan"), None),
        P(("grp", "sub")),
        P(("grp", "sub")),
        P(("grp", "sub"), None),
        P(("grp", "sub"), None),
        P("chan", ("grp", "sub"), None, None),
    )
    out_specs = P("chan", ("grp", "sub"), None, None)
    return jax.shard_map(local, mesh=mesh, in_specs=in_specs, out_specs=out_specs, check_vma=False)
```

```python
import functools
import math

import jax
import jax.numpy as jnp
import numpy as np
from jax import lax
from jax.experimental import pallas as pl
from jax.experimental.pallas import tpu as pltpu
from jax.sharding import PartitionSpec as P

SUB = 32
LANES = 128
SLOTS = LANES // SUB
QROWS = SUB // SLOTS
ROWS = 2 * SUB + 16
STEP = 16
SINE = (3.14159027, -5.16740673, 2.54401052, -0.55946246)
COSINE = (0.99999325, -4.93393467, 4.0412481, -1.22203176)
SINE_LONG = (3.14159264, -5.16771008, 2.55007752, -0.59829129, 0.07765766)
COSINE_LONG = (0.99999995, -4.93479283, 4.05841135, -1.33187657, 0.21968961)


def series(terms, square):
    value = terms[-1]
    for term in terms[-2::-1]:
        value = term + square * value
    return value


def turn_cos_sin(turns, sine_terms=SINE_LONG, cosine_terms=COSINE_LONG):
    part = turns - jnp.round(turns)
    square = part * part
    sine = part * series(sine_terms, square)
    twice = sine + sine
    return 1.0 - twice * sine, twice * series(cosine_terms, square)


def times(a_real, a_imag, b_real, b_imag):
    return a_real * b_real - a_imag * b_imag, a_real * b_imag + a_imag * b_real


def iota(shape, axis):
    return lax.broadcasted_iota(jnp.int32, shape, axis)


def pixel_lines():
    lane = iota((QROWS, LANES), 1)
    return iota((QROWS, LANES), 0) * SLOTS + lane // SUB - SUB // 2, lane % SUB - SUB // 2


def image_kernel(
    axis_size, used_hbm, row_hbm, pair_hbm, vis_hbm, tracks_hbm, freq_hbm, offset_hbm, table_hbm, *rest
):
    send_refs, (centre_ref, table_ref), scratch = rest[:-18], rest[-18:-16], rest[-16:]
    (used_ref, row_ref, pair_ref, vis_ref, tracks_ref, freq_ref, lines_ref, turns_ref, powers_ref, total_ref,
     sems, wide_ref, image_ref, sums_ref, block_ref, offset_ref) = scratch
    base_count, blocks, _, samples = vis_ref.shape
    channels = freq_ref.shape[1]
    steps = samples // channels
    groups = -(-base_count // SLOTS)
    me = lax.axis_index("sub")
    lines = 2 * base_count
    tiles = samples // LANES
    sources = (
        (tracks_hbm, tracks_ref), (freq_hbm, freq_ref), (used_hbm, used_ref), (vis_hbm.at[0], vis_ref),
        (row_hbm, row_ref), (pair_hbm, pair_ref), (offset_hbm, offset_ref),
        (table_hbm, table_ref),
    )
    copies = [pltpu.make_async_copy(one, two, sems.at[n]) for n, (one, two) in enumerate(sources)]
    for copy in copies:
        copy.start()
    total_ref[...] = jnp.zeros_like(total_ref)
    sums_ref[...] = jnp.zeros_like(sums_ref)
    wide_ref[...] = jnp.zeros_like(wide_ref)

    copies[0].wait()
    copies[1].wait()
    for b in range(base_count):
        lines_ref[2 * b : 2 * b + 2, :] = tracks_ref[b]
    wide_ref[0:1, :channels] = freq_ref[...]
    wide = jnp.broadcast_to(wide_ref[0:1, :], (8, LANES))
    lane = iota((8, LANES), 1)
    ratio = jnp.concatenate(
        [jnp.take_along_axis(wide, (lane + m * LANES) // steps, axis=1) for m in range(tiles)], axis=1
    )[0:1] * (1.0 / SUB)
    weight = jnp.where(iota((lines, 1), 0) % 2 == 0, 1.0, float(QROWS))

    def prepare(j, _):
        moved = jnp.take_along_axis(lines_ref[...], iota((lines, LANES), 1) % steps + j * steps, axis=1)
        turns = jnp.concatenate([moved] * tiles, axis=1) * ratio
        turns = turns - jnp.round(turns)
        turns_ref[j] = turns
        one = turn_cos_sin(turns * weight, SINE, COSINE)
        two = times(*one, *one)
        for power, (real, imag) in enumerate((one, two)):
            powers_ref[j, 2 * power] = real
            powers_ref[j, 2 * power + 1] = imag
        return 0

    lax.fori_loop(0, blocks, prepare, 0, unroll=blocks if lines <= 8 else 1)
    q_start = (iota((QROWS, 1), 0) * SLOTS - SUB // 2).astype(jnp.float32)
    r_start = iota((QROWS, 1), 0).astype(jnp.float32) + 0.5
    for copy in copies[2:-1]:
        copy.wait()

    q, r = pixel_lines()
    line = lambda h: 1.0 - (2.0 * h.astype(jnp.float32) / (SUB + 2)) ** 2
    taper = line(q) * line(r)
    for slot in range(base_count):
        turn = lax.rem(offset_ref[0, slot] * q + offset_ref[1, slot] * r, SUB)
        cosine, sine = turn_cos_sin(turn.astype(jnp.float32) * (1.0 / SUB))
        centre_ref[slot, 0] = cosine * taper
        centre_ref[slot, 1] = -sine * taper

    count = jnp.int32(0)
    for b in range(base_count):

        def note(j, _):
            block_ref[count + j] = b * blocks + j
            return 0

        lax.fori_loop(0, used_ref[b], note, 0)
        count = count + used_ref[b]
    for n in range(STEP - 1):
        block_ref[count + n] = 0

    def some_blocks(step, _):
        for n in range(STEP):
            block = block_ref[step * STEP + n]
            b, j = block // blocks, block % blocks
            sample = vis_ref[b, j].astype(jnp.float32)
            sample = jnp.where(step * STEP + n < count, sample, 0.0)

            def power(n, line):
                return powers_ref[j, 2 * n, pl.ds(line, 1), :], powers_ref[j, 2 * n + 1, pl.ds(line, 1), :]

            turns = [turns_ref[j, pl.ds(2 * b + axis, 1), :] for axis in range(2)]
            one = power(0, 2 * b)
            first = turn_cos_sin(turns[0] * q_start - turns[1] * 0.5, SINE, COSINE)
            first = times(*first, sample[0:1], sample[1:2])
            third = times(*first, *power(1, 2 * b))
            left = [first, times(*first, *one), third, times(*third, *one)]
            first = turn_cos_sin(turns[1] * r_start, SINE, COSINE)
            right = [first, times(*first, *power(0, 2 * b + 1))]
            left, right = (
                jnp.concatenate([pair[c] for c in range(2) for pair in pairs], axis=0).astype(jnp.bfloat16)
                for pairs in (left, right)
            )
            sums_ref[b] += lax.dot_general(left, right, (((1,), (1,)), ((), ())), preferred_element_type=jnp.float32)
        return 0

    lax.fori_loop(0, (count + STEP - 1) // STEP, some_blocks, 0)
    for b in range(base_count):
        image_ref[0 : 2 * SUB, 0:SUB] = sums_ref[b] * samples**-0.5
        stations = iota((ROWS - 2 * SUB, LANES), 0)
        stations = jnp.where(stations == 0, pair_ref[0, b], jnp.where(stations == 1, pair_ref[1, b], 0))
        image_ref[2 * SUB :, :] = stations.astype(jnp.float32)
        image = jnp.where(iota((ROWS, LANES), 1) < SUB, image_ref[...], 0.0)
        row = row_ref[b]
        owner = row // base_count
        slot = row % base_count
        place = lax.rem(owner - me + axis_size, axis_size)
        total_ref[place, slot // SLOTS] += pltpu.roll(image, (slot % SLOTS) * SUB, 1)
    if len(send_refs) > 1:
        for place, send_ref in enumerate(send_refs):
            send_ref[...] = total_ref[place].astype(jnp.bfloat16)
    else:
        send_refs[0][...] = total_ref[...].astype(jnp.bfloat16)
    copies[-1].wait()


def split_rows(value, rows_ref, first):
    for a in range(value.shape[1] // LANES):
        rows_ref[first + 2 * a : first + 2 * a + 2, :] = value[:, a * LANES : (a + 1) * LANES]


def halves(value):
    high = value.astype(jnp.bfloat16)
    return high, (value - high.astype(jnp.float32)).astype(jnp.bfloat16)


def swap(parts, lane):
    swapped = []
    for s in range(SLOTS):
        value = parts[s]
        for i in range(SLOTS):
            if i != s:
                value = jnp.where(lane // SUB == i, pltpu.roll(parts[i], ((i - s) % SLOTS) * SUB, 1), value)
        swapped.append(value)
    return swapped


def subgrid_kernel(centre_ref, *rest):
    payload_refs, (pixels_ref, station_ref) = rest[:-2], rest[-2:]
    lane = iota((QROWS, LANES), 1)
    size = (LANES, LANES)
    column, pixel = iota(size, 0) % SUB, iota(size, 1) % SUB
    same = iota(size, 0) // SUB == iota(size, 1) // SUB
    above = same & (pixel - SUB // 2 == column % (SUB // 2))
    below = same & (SUB // 2 - 1 - pixel == column % (SUB // 2))
    even = jnp.where((above | below) & (column < SUB // 2), 1.0, 0.0)
    odd = jnp.where(column < SUB // 2, 0.0, jnp.where(below, 1.0, jnp.where(above, -1.0, 0.0)))
    unfold = jnp.concatenate([even, odd], axis=1).astype(jnp.bfloat16)
    for g in range(pixels_ref.shape[0] // SLOTS):
        parts = []
        for ref in payload_refs:
            parts += [ref[g]] if len(ref.shape) == 3 else [ref[p, g] for p in range(ref.shape[0])]
        whole = parts[0].astype(jnp.float32)
        for part in parts[1:]:
            whole = whole + part.astype(jnp.float32)
        full = jnp.dot(whole[: 2 * SUB].astype(jnp.bfloat16), unfold, preferred_element_type=jnp.float32)
        real = full[:SUB, :LANES] + full[SUB:, LANES:]
        imag = full[SUB:, :LANES] - full[:SUB, LANES:]
        station_ref[g] = whole[2 * SUB : 2 * SUB + 8].astype(jnp.int32)
        real = swap([real[i * QROWS : (i + 1) * QROWS] for i in range(SLOTS)], lane)
        imag = swap([imag[i * QROWS : (i + 1) * QROWS] for i in range(SLOTS)], lane)
        for s in range(SLOTS):
            slot = g * SLOTS + s
            pixels_ref[slot, 0], pixels_ref[slot, 1] = times(real[s], imag[s], centre_ref[slot, 0], centre_ref[slot, 1])


def finish_kernel(table_ref, station_ref, pixels_ref, *rest):
    screens_refs, (out_ref, screen_ref) = rest[:-2], rest[-2:]
    second = table_ref.shape[0] // 2
    me = lax.axis_index("sub")
    lane = iota((QROWS, LANES), 1)

    def screen(station):
        if len(screens_refs) == 1:
            return screens_refs[0][0, station]
        here = screens_refs[0].shape[1]
        away = me ^ (station // here)
        value = screens_refs[0][0, station % here].astype(jnp.float32)
        for flips in range(1, len(screens_refs)):
            value = jnp.where(away == flips, screens_refs[flips][0, station % here].astype(jnp.float32), value)
        return value

    for g in range(pixels_ref.shape[0] // SLOTS):
        weighted = []
        names = station_ref[g]
        for s in range(SLOTS):
            slot = g * SLOTS + s
            pair = []
            for e in range(2):
                n = 2 * s + e
                split_rows(screen(names[e, s * SUB]).astype(jnp.float32), screen_ref.at[n], 0)
                pair.append((screen_ref[n, pl.ds(0, QROWS, stride=2), :], screen_ref[n, pl.ds(1, QROWS, stride=2), :]))
            (p_real, p_imag), (s_real, s_imag) = pair
            gain = times(p_real, -p_imag, s_real, s_imag)
            weighted.append(times(pixels_ref[slot, 0], pixels_ref[slot, 1], *gain))
        planes = swap([pair[0] for pair in weighted], lane) + swap([pair[1] for pair in weighted], lane)
        planes = jnp.concatenate(planes, axis=0)
        high, low = halves(planes)
        wide = jnp.dot(jnp.concatenate([high, low], axis=0), table_ref[:LANES], preferred_element_type=jnp.float32)
        half = wide[: 2 * SUB] + wide[2 * SUB :]
        half = half + jnp.dot(high, table_ref[second : second + LANES], preferred_element_type=jnp.float32)
        half_real = half[:SUB, :LANES] + half[SUB:, LANES:]
        half_imag = half[SUB:, :LANES] - half[:SUB, LANES:]
        half = jnp.concatenate([half_real, half_imag], axis=0)
        high, low = halves(half)
        q_high = table_ref[LANES:second, : 2 * SUB]
        q_low = table_ref[second + LANES :, : 2 * SUB]
        wide = jnp.dot(q_high, jnp.concatenate([high, low], axis=1), preferred_element_type=jnp.float32)
        full = wide[:, :LANES] + wide[:, LANES:] + jnp.dot(q_low, high, preferred_element_type=jnp.float32)
        for c in range(2):
            flat = swap([full[c * SUB + i * QROWS : c * SUB + (i + 1) * QROWS] for i in range(SLOTS)], lane)
            for s in range(SLOTS):
                for a in range(QROWS):
                    out_ref[0, g * SLOTS + s, c : c + 1, a * LANES : (a + 1) * LANES] = flat[s][a : a + 1]


def tables():
    h = [n - SUB // 2 for n in range(SUB)]
    order = [(n % QROWS) * SLOTS + n // QROWS - SUB // 2 for n in range(SUB)]
    turn = lambda f, x, y: f(2.0 * math.pi * ((x * y) % SUB) / SUB)
    r_table = [
        [turn(f, h[m % SUB], h[n % SUB]) if m // SUB == n // SUB else 0.0 for f in (math.cos, math.sin) for n in range(LANES)]
        for m in range(LANES)
    ]
    cos = [[turn(math.cos, x, y) / SUB for y in order] for x in order]
    sin = [[turn(math.sin, x, y) / SUB for y in order] for x in order]
    q_table = [c + s for c, s in zip(cos, sin)] + [[-v for v in s] + c for c, s in zip(cos, sin)]
    table = np.array(r_table + [row + [0.0] * (2 * LANES - 2 * SUB) for row in q_table], np.float32)
    high = table.astype(jnp.bfloat16)
    return jnp.array(np.concatenate([high, (table - high.astype(np.float32)).astype(jnp.bfloat16)], axis=0))


def local(
    visibilities, tracks, freq_ratio, blocks_used, subgrid_row, station_pair, subgrid_offsets, aterm_screens
):
    owners = lax.axis_size("sub")
    base_count, blocks, _, samples = visibilities.shape[1:]
    groups = -(-base_count // SLOTS)
    here, _, pixels = aterm_screens.shape[1:]
    vmem = pl.BlockSpec(memory_space=pltpu.VMEM)
    hbm = pl.BlockSpec(memory_space=pltpu.HBM)
    keep = lambda x: pltpu.with_memory_space_constraint(x, pltpu.HBM)
    shift_by = lambda x, shift: lax.ppermute(x, "sub", [(n, (n + shift) % owners) for n in range(owners)])
    direct = owners == 4
    if direct:
        flip = lambda x, bits: lax.ppermute(x, "sub", [(n, n ^ bits) for n in range(owners)])
        screens = [aterm_screens, flip(aterm_screens, 1), flip(aterm_screens, 2)]
        sends = [jax.ShapeDtypeStruct((groups, ROWS, LANES), jnp.bfloat16)] * owners
    else:
        sends = [jax.ShapeDtypeStruct((owners, groups, ROWS, LANES), jnp.bfloat16)]
    sends.append(jax.ShapeDtypeStruct((base_count, 2, QROWS, LANES), jnp.float32))
    sends.append(jax.ShapeDtypeStruct((2 * (LANES + 2 * SUB), 2 * LANES), jnp.bfloat16))
    *sent, centre, table = pl.pallas_call(
        functools.partial(image_kernel, owners),
        out_shape=sends,
        in_specs=[hbm] * 8,
        out_specs=[vmem] * len(sends),
        scratch_shapes=[
            pltpu.SMEM((base_count,), jnp.int32),
            pltpu.SMEM((base_count,), jnp.int32),
            pltpu.SMEM((2, base_count), jnp.int32),
            pltpu.VMEM(visibilities.shape[1:], jnp.bfloat16),
            pltpu.VMEM(tracks.shape, jnp.float32),
            pltpu.VMEM(freq_ratio.shape, jnp.float32),
            pltpu.VMEM((2 * base_count, tracks.shape[-1]), jnp.float32),
            pltpu.VMEM((blocks, 2 * base_count, samples), jnp.float32),
            pltpu.VMEM((blocks, 4, 2 * base_count, samples), jnp.float32),
            pltpu.VMEM((owners, groups, ROWS, LANES), jnp.float32),
            pltpu.SemaphoreType.DMA((8,)),
            pltpu.VMEM((8, LANES), jnp.float32),
            pltpu.VMEM((ROWS, LANES), jnp.float32),
            pltpu.VMEM((base_count, 2 * SUB, SUB), jnp.float32),
            pltpu.SMEM((base_count * blocks + STEP - 1,), jnp.int32),
            pltpu.SMEM((2, base_count), jnp.int32),
        ],
        compiler_params=pltpu.CompilerParams(vmem_limit_bytes=48 * 1024 * 1024),
        name="images",
    )(*map(keep, (blocks_used, subgrid_row, station_pair.T, visibilities, tracks, freq_ratio, subgrid_offsets.T, tables())))
    if direct:
        payloads = [sent[0]] + [shift_by(sent[shift], shift) for shift in (3, 1, 2)]
        payloads[0], screens[2] = lax.optimization_barrier((payloads[0], screens[2]))
        screens.append(flip(screens[2], 1))
        payloads[0], screens[1] = lax.optimization_barrier((payloads[0], screens[1]))
    else:
        by_owner = jnp.roll(sent[0], lax.axis_index("sub"), axis=0)
        payloads = [lax.all_to_all(by_owner, "sub", 0, 0, tiled=True)]
        screens = [lax.all_gather(aterm_screens, "sub", axis=1, tiled=True)]
    subgrids, stations = pl.pallas_call(
        subgrid_kernel,
        out_shape=[
            jax.ShapeDtypeStruct((base_count, 2, QROWS, LANES), jnp.float32),
            jax.ShapeDtypeStruct((groups, 8, LANES), jnp.int32),
        ],
        in_specs=[vmem] * (1 + len(payloads)),
        out_specs=[vmem] * 2,
        compiler_params=pltpu.CompilerParams(vmem_limit_bytes=48 * 1024 * 1024),
        cost_estimate=pl.CostEstimate(flops=10000000000, bytes_accessed=100000, transcendentals=0),
        name="subgrids",
    )(centre, *payloads)
    return pl.pallas_call(
        finish_kernel,
        out_shape=jax.ShapeDtypeStruct((1, base_count, 2, pixels), jnp.float32),
        in_specs=[vmem] * (3 + len(screens)),
        out_specs=vmem,
        scratch_shapes=[
            pltpu.VMEM((2 * SLOTS, 2 * QROWS, LANES), jnp.float32),
        ],
        compiler_params=pltpu.CompilerParams(vmem_limit_bytes=48 * 1024 * 1024),
        name="finish",
    )(table, stations, subgrids, *screens)


def solution(mesh):
    in_specs = (
        P("chan", ("grp", "sub"), None, None, None),
        P(("grp", "sub"), None, None),
        P(("grp", "chan"), None),
        P(("grp", "sub")),
        P(("grp", "sub")),
        P(("grp", "sub"), None),
        P(("grp", "sub"), None),
        P("chan", ("grp", "sub"), None, None),
    )
    out_specs = P("chan", ("grp", "sub"), None, None)
    return jax.shard_map(local, mesh=mesh, in_specs=in_specs, out_specs=out_specs, check_vma=False)
```
